512 devices in a mesh: dp: 32 (over x, y, core), tensor: 16 (over z).
Axes of the slice: x: 4, y: 4, z: 16, core: 2. Of those that a mesh axis runs over, the one named last changes fastest.
Arguments:
- grad: bfloat16 [32, 2048, 4096], P('dp', 'tensor'), may hold values from -6 to 6
- error: bfloat16 [32, 2048, 4096], P('dp', 'tensor'), may hold values from -4 to 4
- q_start: bfloat16 [4096, 64], P('tensor'), may hold values from -6 to 6
Outputs:
- update: bfloat16 [2048, 4096], P('tensor')
- new_error: bfloat16 [32, 2048, 4096], P('dp', 'tensor')
- q_new: float32 [4096, 64], P('tensor')
The draws below stay inside these ranges and needn't reach their ends.
All inputs are finite; a program needn't handle non-finite values.
Results may differ from the reference program's by a relative error of at most 0.012.
Values may be sent and summed in bfloat16 or wider, within the bound.
No kernel may reach another device: no remote copies, remote signals or barrier semaphores. Data moves between devices by JAX's collectives and lax.ppermute only.
A program may use at most 64 MiB of HBM per device.

```python
import jax
import jax.numpy as jnp
from jax import lax

D = 4096
R = 64
ROWS = 2048
REPLICAS = 32


def shard_levels(own_key, extent, cuts, smallest, largest):
    loudness = 1.0
    for position, blocks in cuts:
        heights = jax.random.uniform(jax.random.fold_in(jax.random.fold_in(own_key, 6), position), (blocks,), jnp.float32, smallest / len(cuts), largest / len(cuts))
        loudness = loudness * jnp.repeat(jnp.exp(heights), extent[position] // blocks).reshape((-1,) + (1,) * (len(extent) - 1 - position))
    return loudness


def gaussian(rng, dims, spread, bound, cuts=(), held_as=jnp.bfloat16):
    loudness = shard_levels(rng, dims, cuts, -0.22, 0.18) if cuts else 1.0
    result = jax.random.normal(rng, dims, jnp.float32) * spread * loudness
    return jnp.minimum(jnp.maximum(result, -bound), bound).astype(held_as)


def setup_inputs(seed: int = 0) -> dict:
    seeds = jax.random.split(jax.random.key(seed), 4)
    grad = gaussian(seeds[0], (REPLICAS, ROWS, D), 1.0, 6.0, ((0, 32), (1, 16)))
    error = gaussian(seeds[1], (REPLICAS, ROWS, D), 0.5, 4.0, ((0, 32), (1, 16)))
    q_start = gaussian(seeds[2], (D, R), 1.0, 6.0, ((0, 16),))
    return {"grad": grad, "error": error, "q_start": q_start}


def correct_one(grad_one, error_one):
    return (grad_one.astype(jnp.float32) + error_one.astype(jnp.float32)).astype(jnp.bfloat16)

def reference(grad, error, q_start):

    def sketch_step(total, pair):
        corrected = correct_one(pair[0], pair[1])
        return (total + jnp.dot(corrected.astype(jnp.float32), q_start.astype(jnp.float32), preferred_element_type=jnp.float32), None)
    p_sum, unused = lax.scan(sketch_step, jnp.zeros((grad.shape[1], q_start.shape[1]), jnp.float32), (grad, error))
    gram = jnp.dot(p_sum.T, p_sum, precision=lax.Precision.HIGHEST)
    lower = lax.linalg.cholesky(gram)
    p_hat = lax.linalg.triangular_solve(lower, p_sum, left_side=False, lower=True, transpose_a=True)
    p_round = p_hat.astype(jnp.bfloat16)

    def basis_step(total, pair):
        corrected = correct_one(pair[0], pair[1])
        term = lax.dot_general(corrected.astype(jnp.float32), p_round.astype(jnp.float32), (((0,), (0,)), ((), ())), preferred_element_type=jnp.float32)
        return (total + term, None)
    q_total, unused = lax.scan(basis_step, jnp.zeros((grad.shape[2], q_start.shape[1]), jnp.float32), (grad, error))
    q_new = q_total / REPLICAS
    q_round = q_new.astype(jnp.bfloat16)
    full_update = lax.dot_general(p_round.astype(jnp.float32), q_round.astype(jnp.float32), (((1,), (1,)), ((), ())), preferred_element_type=jnp.float32)

    def error_one(pair):
        corrected = correct_one(pair[0], pair[1])
        return (corrected.astype(jnp.float32) - full_update).astype(jnp.bfloat16)
    new_error = lax.map(error_one, (grad, error))
    return (full_update.astype(jnp.bfloat16), new_error, q_new)
```

```python
import jax
import jax.numpy as jnp
from jax import lax
from jax.sharding import PartitionSpec as P

SIDE = 4
CHIPS = SIDE * SIDE
CORES = 2
DP = CHIPS * CORES
DEPTH = 16
R = 64
HIGH = lax.Precision.HIGHEST

PLANE = [[core + CORES * chip for chip in range(CHIPS)] for core in range(CORES)]
NEAR = [[4 * a + b for b in range(4)] for a in range(4)]
FAR = [[4 * a + b for a in range(4)] for b in range(4)]
SWAP = [(i, i ^ 1) for i in range(DP)]


def ring(a, b, n):
    return min((a - b) % n, (b - a) % n)


def factor_route():
    pairs = []
    for k in range(CHIPS):
        planes = sorted(range(DEPTH), key=lambda z: -ring(z, k, DEPTH))
        chips = sorted(
            range(CHIPS),
            key=lambda j: ring(j // SIDE, k // SIDE, SIDE) + ring(j % SIDE, k % SIDE, SIDE),
        )
        for z, j in zip(planes, chips):
            for core in range(CORES):
                pairs.append(((CORES * j + core) * DEPTH + k, (CORES * k + core) * DEPTH + z))
    return pairs


def share(x, axis, groups, size):
    return lax.all_to_all(
        jnp.broadcast_to(x[None], (size,) + x.shape), axis, 0, 0, axis_index_groups=groups
    )


def body(grad, error, q_start):
    core = lax.axis_index("dp") % CORES
    z = lax.axis_index("tensor")
    factor_t = lax.ppermute(q_start.T, ("dp", "tensor"), factor_route())
    corrected = (grad[0].astype(jnp.float32) + error[0].astype(jnp.float32)).astype(jnp.bfloat16)
    blocks = corrected.reshape(CORES, 64, CHIPS, 256).transpose(2, 0, 1, 3).reshape(DP, 64, 256)
    blocks = lax.all_to_all(blocks, "dp", 0, 0)
    total = jnp.sum(blocks.astype(jnp.float32), 0)
    part = lax.dot_general(
        total, factor_t.astype(jnp.float32), (((1,), (1,)), ((), ())), precision=HIGH
    )
    part = jnp.concatenate([part[:32], part[32:]], 1)
    packed_p = jnp.sum(share(part, "dp", PLANE, CHIPS), 0)
    p_mine = jnp.concatenate([packed_p[:, :R], packed_p[:, R:]], 0)
    t_part = lax.dot_general(p_mine, total, (((0,), (0,)), ((), ())), precision=HIGH)
    gram = lax.dot_general(p_mine, p_mine, (((0,), (0,)), ((), ())), precision=HIGH)
    gram = jnp.concatenate([gram[:32], gram[32:]], 1)
    keep = lax.dynamic_slice_in_dim(t_part, core * 128, 128, 1)
    give = lax.dynamic_slice_in_dim(t_part, (1 - core) * 128, 128, 1)
    got = lax.ppermute(jnp.concatenate([give, gram, packed_p], 0), "dp", SWAP)
    other_p = jnp.concatenate([got[96:, :R], got[96:, R:]], 0)
    p_sum = jnp.where(
        core == 0,
        jnp.concatenate([p_mine, other_p], 0),
        jnp.concatenate([other_p, p_mine], 0),
    )
    both = jnp.concatenate([keep, gram], 0) + got[:96]
    both = jnp.sum(share(both, "tensor", NEAR, 4), 0)
    both = jnp.sum(share(both, "tensor", FAR, 4), 0)
    gram = jnp.concatenate([both[64:, :R], both[64:, R:]], 0)
    lower = lax.linalg.cholesky(gram)
    inverse = lax.linalg.triangular_solve(
        lower, jnp.eye(R, dtype=jnp.float32), left_side=True, lower=True
    )
    q_block = jnp.dot(inverse, both[:64], precision=HIGH) / DP
    p_round = lax.dot_general(
        p_sum, inverse, (((1,), (1,)), ((), ())), precision=HIGH
    ).astype(jnp.bfloat16)
    q_blocks = share(q_block.astype(jnp.bfloat16), "dp", None, DP)
    q_round = q_blocks.transpose(1, 0, 2).reshape(R, DP * 128)
    full_update = jnp.dot(p_round, q_round, preferred_element_type=jnp.float32)
    new_error = (corrected.astype(jnp.float32) - full_update).astype(jnp.bfloat16)[None]
    q_mine = lax.dynamic_slice_in_dim(q_blocks, z * 2, 2, 0)
    q_mine = q_mine.transpose(0, 2, 1).reshape(256, R).astype(jnp.float32)
    return (full_update.astype(jnp.bfloat16), new_error, q_mine)


def solution(mesh):
    placed = (P("dp", "tensor", None), P("dp", "tensor", None), P("tensor", None))
    return jax.shard_map(
        body,
        mesh=mesh,
        in_specs=placed,
        out_specs=(P("tensor", None), P("dp", "tensor", None), P("tensor", None)),
        check_vma=False,
    )
```

```python
import jax
import jax.numpy as jnp
from jax import lax
from jax.experimental import pallas as pl
from jax.sharding import PartitionSpec as P

SIDE = 4
CHIPS = SIDE * SIDE
CORES = 2
DP = CHIPS * CORES
DEPTH = 16
R = 64
HIGH = lax.Precision.HIGHEST

PLANE = [[core + CORES * chip for chip in range(CHIPS)] for core in range(CORES)]
NEAR = [[4 * a + b for b in range(4)] for a in range(4)]
FAR = [[4 * a + b for a in range(4)] for b in range(4)]
SWAP = [(i, i ^ 1) for i in range(DP)]


def ring(a, b, n):
    return min((a - b) % n, (b - a) % n)


def factor_route():
    pairs = []
    for k in range(CHIPS):
        planes = sorted(range(DEPTH), key=lambda z: -ring(z, k, DEPTH))
        chips = sorted(
            range(CHIPS),
            key=lambda j: ring(j // SIDE, k // SIDE, SIDE) + ring(j % SIDE, k % SIDE, SIDE),
        )
        for z, j in zip(planes, chips):
            for core in range(CORES):
                pairs.append(((CORES * j + core) * DEPTH + k, (CORES * k + core) * DEPTH + z))
    return pairs


def share(x, axis, groups, size):
    return lax.all_to_all(
        jnp.broadcast_to(x[None], (size,) + x.shape), axis, 0, 0, axis_index_groups=groups
    )


def splat_row(x, row):
    return jnp.broadcast_to(x[row : row + 1, :], (8, 128))


def inverse_factor(gram):
    rows = lax.broadcasted_iota(jnp.int32, (R, R), 0)
    eye = (rows == lax.broadcasted_iota(jnp.int32, (R, R), 1)).astype(jnp.float32)
    both = jnp.concatenate([gram, eye], 1)
    n = R // 8
    strips = [both[8 * t : 8 * t + 8] for t in range(n)]
    sub = lax.broadcasted_iota(jnp.int32, (8, 128), 0)
    scaled = []
    for s in range(n):
        cols = [
            [jnp.broadcast_to(strips[t][:, 8 * s + j : 8 * s + j + 1], (8, 128)) for t in range(s, n)]
            for j in range(8)
        ]
        done = jnp.zeros((8, 128), jnp.float32)
        for j in range(8):
            pivot, row = splat_row(cols[j][0], j), splat_row(strips[s], j)
            root = lax.rsqrt(pivot)
            root = root * (1.5 - 0.5 * pivot * root * root)
            done = jnp.where(sub == j, row * root, done)
            factors = [c * (root * root) for c in cols[j]]
            factors[0] = jnp.where(sub > j, factors[0], 0.0)
            for i in range(j + 1, 8):
                entry = splat_row(cols[i][0], j)
                cols[i] = [c - f * entry for c, f in zip(cols[i], factors)]
            for t in range(s, n):
                strips[t] = strips[t] - factors[t - s] * row
        scaled.append(done)
    return jnp.concatenate(scaled, 0)[:, R:]


def factor_kernel(far_ref, p_ref, q_ref, p_round_ref):
    both = far_ref[0] + far_ref[1] + (far_ref[2] + far_ref[3])
    inverse = inverse_factor(jnp.concatenate([both[64:, :R], both[64:, R:]], 0))
    q_block = jnp.dot(
        inverse, both[:64], precision=HIGH, preferred_element_type=jnp.float32
    ) * (1.0 / DP)
    q_ref[...] = jnp.broadcast_to(q_block.astype(jnp.bfloat16)[None], q_ref.shape)
    p_round_ref[...] = lax.dot_general(
        p_ref[...],
        inverse,
        (((1,), (1,)), ((), ())),
        precision=HIGH,
        preferred_element_type=jnp.float32,
    ).astype(jnp.bfloat16)


def body(grad, error, q_start):
    core = lax.axis_index("dp") % CORES
    z = lax.axis_index("tensor")
    factor_t = lax.ppermute(q_start.T, ("dp", "tensor"), factor_route())
    corrected = (grad[0].astype(jnp.float32) + error[0].astype(jnp.float32)).astype(jnp.bfloat16)
    blocks = corrected.reshape(CORES, 64, CHIPS, 256).transpose(2, 0, 1, 3).reshape(DP, 64, 256)
    blocks = lax.all_to_all(blocks, "dp", 0, 0)
    total = jnp.sum(blocks.astype(jnp.float32), 0)
    part = lax.dot_general(
        total, factor_t.astype(jnp.float32), (((1,), (1,)), ((), ())), precision=HIGH
    )
    part = jnp.concatenate([part[:32], part[32:]], 1)
    packed_p = jnp.sum(share(part, "dp", PLANE, CHIPS), 0)
    p_mine = jnp.concatenate([packed_p[:, :R], packed_p[:, R:]], 0)
    t_part = lax.dot_general(p_mine, total, (((0,), (0,)), ((), ())), precision=HIGH)
    gram = lax.dot_general(p_mine, p_mine, (((0,), (0,)), ((), ())), precision=HIGH)
    gram = jnp.concatenate([gram[:32], gram[32:]], 1)
    keep = lax.dynamic_slice_in_dim(t_part, core * 128, 128, 1)
    give = lax.dynamic_slice_in_dim(t_part, (1 - core) * 128, 128, 1)
    got = lax.ppermute(jnp.concatenate([give, gram, packed_p], 0), "dp", SWAP)
    other_p = jnp.concatenate([got[96:, :R], got[96:, R:]], 0)
    p_sum = jnp.where(
        core == 0,
        jnp.concatenate([p_mine, other_p], 0),
        jnp.concatenate([other_p, p_mine], 0),
    )
    both = jnp.concatenate([keep, gram], 0) + got[:96]
    both = jnp.sum(share(both, "tensor", NEAR, 4), 0)
    q_blocks, p_round = pl.pallas_call(
        factor_kernel,
        out_shape=(
            jax.ShapeDtypeStruct((DP, R, 128), jnp.bfloat16),
            jax.ShapeDtypeStruct((128, R), jnp.bfloat16),
        ),
    )(share(both, "tensor", FAR, 4), p_sum)
    q_blocks = lax.all_to_all(q_blocks, "dp", 0, 0)
    q_round = q_blocks.transpose(1, 0, 2).reshape(R, DP * 128)
    full_update = jnp.dot(p_round, q_round, preferred_element_type=jnp.float32)
    new_error = (corrected.astype(jnp.float32) - full_update).astype(jnp.bfloat16)[None]
    q_mine = lax.dynamic_slice_in_dim(q_blocks, z * 2, 2, 0)
    q_mine = q_mine.transpose(0, 2, 1).reshape(256, R).astype(jnp.float32)
    return (full_update.astype(jnp.bfloat16), new_error, q_mine)


def solution(mesh):
    placed = (P("dp", "tensor", None), P("dp", "tensor", None), P("tensor", None))
    return jax.shard_map(
        body,
        mesh=mesh,
        in_specs=placed,
        out_specs=(P("tensor", None), P("dp", "tensor", None), P("tensor", None)),
        check_vma=False,
    )
```

```python
import jax
import jax.numpy as jnp
from jax import lax
from jax.experimental import pallas as pl
from jax.experimental.pallas import tpu as pltpu
from jax.sharding import PartitionSpec as P

SIDE = 4
CHIPS = SIDE * SIDE
CORES = 2
DP = CHIPS * CORES
DEPTH = 16
ROWS = 128
HALF = ROWS // CORES
D = 4096
COLS = D // CHIPS
R = 64
HIGH = lax.Precision.HIGHEST
F32, BF16 = jnp.float32, jnp.bfloat16

PLANE = [[core + CORES * chip for chip in range(CHIPS)] for core in range(CORES)]
NEAR = [[4 * a + b for b in range(4)] for a in range(4)]
FAR = [[4 * a + b for a in range(4)] for b in range(4)]
SWAP = [(i, i ^ 1) for i in range(DP)]
PAIRED = [[i * DEPTH + 2 * a + b for b in range(2) for i in range(DP)] for a in range(DEPTH // 2)]


def ring(a, b, n):
    return min((a - b) % n, (b - a) % n)


def factor_route():
    pairs = []
    for k in range(CHIPS):
        planes = sorted(range(DEPTH), key=lambda z: -ring(z, k, DEPTH))
        chips = sorted(
            range(CHIPS),
            key=lambda j: ring(j // SIDE, k // SIDE, SIDE) + ring(j % SIDE, k % SIDE, SIDE),
        )
        for z, j in zip(planes, chips):
            for core in range(CORES):
                pairs.append(((CORES * j + core) * DEPTH + k, (CORES * k + core) * DEPTH + z))
    return pairs


def shape(*dims, dtype=F32):
    return jax.ShapeDtypeStruct(dims, dtype)


def pack(x):
    return jnp.concatenate([x[:32, :R], x[32:, :R]], 1)


def unpack(x):
    return jnp.concatenate([x[:, :R], x[:, R:]], 0)


def dot(a, b, over, **kw):
    return lax.dot_general(a, b, (over, ((), ())), preferred_element_type=F32, **kw)


def correct_kernel(grad_ref, error_ref, out_ref):
    x = (grad_ref[0].astype(F32) + error_ref[0].astype(F32)).astype(BF16)
    for k in range(out_ref.shape[0] // CORES):
        for c in range(CORES):
            out_ref[CORES * k + c] = x[HALF * c : HALF * (c + 1), COLS * k : COLS * (k + 1)]


def sketch_kernel(blocks_ref, factor_ref, total_ref, share_ref):
    total = blocks_ref[0].astype(F32)
    for i in range(1, DP):
        total = total + blocks_ref[i].astype(F32)
    total_ref[...] = total
    part = pack(dot(total, factor_ref[...].astype(F32), ((1,), (1,)), precision=HIGH))
    share_ref[...] = jnp.broadcast_to(part[None], share_ref.shape)


def basis_kernel(share_ref, total_ref, give_ref, keep_ref):
    packed = share_ref[0]
    for k in range(1, CHIPS):
        packed = packed + share_ref[k]
    p = unpack(packed)
    first = lax.rem(lax.axis_index("dp"), CORES) == 0
    left = dot(p, total_ref[:, :128], ((0,), (0,)), precision=HIGH)
    right = dot(p, total_ref[:, 128:], ((0,), (0,)), precision=HIGH)
    gram = pack(dot(p, p, ((0,), (0,)), precision=HIGH))
    keep_ref[:R] = jnp.where(first, left, right)
    give_ref[:R] = jnp.where(first, right, left)
    for ref in (keep_ref, give_ref):
        ref[R : R + 32] = gram
        ref[R + 32 :] = packed


def near_kernel(keep_ref, got_ref, share_ref, p_ref):
    both = keep_ref[:R] + got_ref[:R]
    gram = keep_ref[R : R + 32] + got_ref[R : R + 32]
    for half in range(2):
        part = pack(both[:, R * half : R * (half + 1)])
        for m in (half, half + 2):
            share_ref[m, :32] = part
            share_ref[m, 32:] = gram
    first = lax.rem(lax.axis_index("dp"), CORES) == 0
    mine, other = unpack(keep_ref[R + 32 :]), unpack(got_ref[R + 32 :])
    p_ref[:HALF] = jnp.where(first, mine, other)
    p_ref[HALF:] = jnp.where(first, other, mine)


def far_kernel(near_ref, share_ref):
    both = near_ref[0] + near_ref[1] + (near_ref[2] + near_ref[3])
    share_ref[...] = jnp.broadcast_to(both[None], share_ref.shape)


def splat_row(x, row):
    return jnp.broadcast_to(x[row : row + 1, :], (8, 128))


def inverse_factor(gram):
    rows = lax.broadcasted_iota(jnp.int32, (R, R), 0)
    eye = (rows == lax.broadcasted_iota(jnp.int32, (R, R), 1)).astype(F32)
    both = jnp.concatenate([gram, eye], 1)
    n = R // 8
    strips = [both[8 * t : 8 * t + 8] for t in range(n)]
    sub = lax.broadcasted_iota(jnp.int32, (8, 128), 0)
    scaled = []
    for s in range(n):
        cols = [
            [jnp.broadcast_to(strips[t][:, 8 * s + j : 8 * s + j + 1], (8, 128)) for t in range(s, n)]
            for j in range(8)
        ]
        done = jnp.zeros((8, 128), F32)
        for j in range(8):
            pivot, row = splat_row(cols[j][0], j), splat_row(strips[s], j)
            root = lax.rsqrt(pivot)
            root = root * (1.5 - 0.5 * pivot * root * root)
            done = jnp.where(sub == j, row * root, done)
            factors = [c * (root * root) for c in cols[j]]
            factors[0] = jnp.where(sub > j, factors[0], 0.0)
            for i in range(j + 1, 8):
                entry = splat_row(cols[i][0], j)
                cols[i] = [c - f * entry for c, f in zip(cols[i], factors)]
            for t in range(s, n):
                strips[t] = strips[t] - factors[t - s] * row
        scaled.append(done)
    return jnp.concatenate(scaled, 0)[:, R:]


def factor_kernel(far_ref, p_ref, q_ref, p_round_ref):
    both = far_ref[0] + far_ref[1] + (far_ref[2] + far_ref[3])
    inverse = inverse_factor(unpack(both[32:]))
    q_half = dot(inverse, unpack(both[:32]), ((1,), (0,)), precision=HIGH) * (1.0 / DP)
    q_ref[...] = jnp.broadcast_to(pack(q_half).astype(BF16)[None], q_ref.shape)
    p_round_ref[...] = dot(p_ref[...], inverse, ((1,), (1,)), precision=HIGH).astype(BF16)


def update_kernel(q_ref, p_ref, blocks_ref, update_ref, error_ref, q_new_ref):
    n = q_ref.shape[1]

    def columns(i):
        even, odd = q_ref[0, i].astype(F32), q_ref[1, i].astype(F32)
        return (
            jnp.concatenate([even[:, :R], odd[:, :R]], 1),
            jnp.concatenate([even[:, R:], odd[:, R:]], 1),
        )

    for k in range(n // CORES):
        pieces = [jnp.concatenate(columns(CORES * k + c), 0) for c in range(CORES)]
        q = jnp.concatenate(pieces, 1).astype(BF16)
        full = dot(p_ref[...], q, ((1,), (0,)))
        span = slice(COLS * k, COLS * (k + 1))
        update_ref[:, span] = full.astype(BF16)
        for c in range(CORES):
            rows = slice(HALF * c, HALF * (c + 1))
            error_ref[0, rows, span] = (blocks_ref[CORES * k + c].astype(F32) - full[rows]).astype(BF16)

    z = lax.axis_index("tensor")
    step = pl.program_id(0)

    @pl.when(step == lax.div(z, n // CORES))
    def _():
        for c in range(CORES):
            upper, lower = columns(CORES * lax.rem(z, n // CORES) + c)
            q_new_ref[:32, 128 * c : 128 * (c + 1)] = upper
            q_new_ref[32:, 128 * c : 128 * (c + 1)] = lower


STEPS = 4


def body(grad, error, q_start):
    wide = pl.BlockSpec((1, ROWS, D // STEPS), lambda j: (0, 0, j))
    tall = pl.BlockSpec((DP // STEPS, HALF, COLS), lambda j: (j, 0, 0))
    factor_t = lax.ppermute(q_start.T, ("dp", "tensor"), factor_route())
    own = pl.pallas_call(
        correct_kernel,
        grid=(STEPS,),
        in_specs=[wide, wide],
        out_specs=tall,
        out_shape=shape(DP, HALF, COLS, dtype=BF16),
    )(grad, error)
    blocks = lax.all_to_all(own, "dp", 0, 0)
    total, part = pl.pallas_call(
        sketch_kernel, out_shape=(shape(HALF, COLS), shape(CHIPS, 32, 128))
    )(blocks, factor_t)
    part = lax.all_to_all(part, "dp", 0, 0, axis_index_groups=PLANE)
    give, keep = pl.pallas_call(basis_kernel, out_shape=(shape(128, 128), shape(128, 128)))(part, total)
    got = lax.ppermute(give, "dp", SWAP)
    near, p_sum = pl.pallas_call(near_kernel, out_shape=(shape(4, 64, 128), shape(ROWS, R)))(keep, got)
    near = lax.all_to_all(near, "tensor", 0, 0, axis_index_groups=NEAR)
    far = pl.pallas_call(far_kernel, out_shape=shape(4, 64, 128))(near)
    far = lax.all_to_all(far, "tensor", 0, 0, axis_index_groups=FAR)
    q_blocks, p_round = pl.pallas_call(
        factor_kernel,
        out_shape=(shape(2 * DP, 32, 128, dtype=BF16), shape(ROWS, R, dtype=BF16)),
    )(far, p_sum)
    q_blocks = lax.all_to_all(q_blocks, ("dp", "tensor"), 0, 0, axis_index_groups=PAIRED)
    update, new_error, q_mine = pl.pallas_call(
        update_kernel,
        grid=(STEPS,),
        in_specs=[
            pl.BlockSpec((2, DP // STEPS, 32, 128), lambda j: (0, j, 0, 0)),
            pl.BlockSpec((ROWS, R), lambda j: (0, 0)),
            tall,
        ],
        out_specs=[
            pl.BlockSpec((ROWS, D // STEPS), lambda j: (0, j)),
            wide,
            pl.BlockSpec((R, COLS), lambda j: (0, 0)),
        ],
        out_shape=(shape(ROWS, D, dtype=BF16), shape(1, ROWS, D, dtype=BF16), shape(R, COLS)),
    )(q_blocks.reshape(2, DP, 32, 128), p_round, own)
    return (update, new_error, q_mine.T)


def solution(mesh):
    placed = (P("dp", "tensor", None), P("dp", "tensor", None), P("tensor", None))
    return jax.shard_map(
        body,
        mesh=mesh,
        in_specs=placed,
        out_specs=(P("tensor", None), P("dp", "tensor", None), P("tensor", None)),
        check_vma=False,
    )
```

```python
import jax
import jax.numpy as jnp
from jax import lax
from jax.experimental import pallas as pl
from jax.experimental.pallas import tpu as pltpu
from jax.sharding import PartitionSpec as P

SIDE = 4
CHIPS = SIDE * SIDE
CORES = 2
DP = CHIPS * CORES
DEPTH = 16
ROWS = 128
HALF = ROWS // CORES
D = 4096
COLS = D // CHIPS
R = 64
PARTS = 4
HIGH = lax.Precision.HIGHEST
F32, BF16 = jnp.float32, jnp.bfloat16

PLANE = [[core + CORES * chip for chip in range(CHIPS)] for core in range(CORES)]
NEAR = [[4 * a + b for b in range(4)] for a in range(4)]
FAR = [[4 * a + b for a in range(4)] for b in range(4)]
SWAP = [(i, i ^ 1) for i in range(DP)]


def ring(a, b, n):
    return min((a - b) % n, (b - a) % n)


def factor_route():
    pairs = []
    for k in range(CHIPS):
        planes = sorted(range(DEPTH), key=lambda z: -ring(z, k, DEPTH))
        chips = sorted(
            range(CHIPS),
            key=lambda j: ring(j // SIDE, k // SIDE, SIDE) + ring(j % SIDE, k % SIDE, SIDE),
        )
        for z, j in zip(planes, chips):
            for core in range(CORES):
                pairs.append(((CORES * j + core) * DEPTH + k, (CORES * k + core) * DEPTH + z))
    return pairs


def shape(*dims, dtype=F32):
    return jax.ShapeDtypeStruct(dims, dtype)


def pack(x):
    return jnp.concatenate([x[:32, :R], x[32:, :R]], 1)


def unpack(x):
    return jnp.concatenate([x[:, :R], x[:, R:]], 0)


def dot(a, b, over, **kw):
    return lax.dot_general(a, b, (over, ((), ())), preferred_element_type=F32, **kw)


def block_kernel(rows_ref, out_ref):
    for k in range(CHIPS):
        for c in range(CORES):
            out_ref[CORES * k + c] = rows_ref[HALF * c : HALF * (c + 1), COLS * k : COLS * (k + 1)]


def sketch_kernel(blocks_ref, factor_ref, total_ref, share_ref):
    total = blocks_ref[0].astype(F32)
    for i in range(1, DP):
        total = total + blocks_ref[i].astype(F32)
    total_ref[...] = total
    part = pack(dot(total, factor_ref[...].astype(F32), ((1,), (1,)), precision=HIGH))
    share_ref[...] = jnp.broadcast_to(part[None], share_ref.shape)


def basis_kernel(share_ref, total_ref, give_ref, keep_ref):
    packed = share_ref[0]
    for k in range(1, CHIPS):
        packed = packed + share_ref[k]
    p = unpack(packed)
    first = lax.rem(lax.axis_index("dp"), CORES) == 0
    left = dot(p, total_ref[:, :128], ((0,), (0,)), precision=HIGH)
    right = dot(p, total_ref[:, 128:], ((0,), (0,)), precision=HIGH)
    gram = pack(dot(p, p, ((0,), (0,)), precision=HIGH))
    keep_ref[:R] = jnp.where(first, left, right)
    give_ref[:R] = jnp.where(first, right, left)
    for ref in (keep_ref, give_ref):
        ref[R : R + 32] = gram
        ref[R + 32 :] = packed


def near_kernel(keep_ref, got_ref, share_ref, p_ref):
    both = keep_ref[: R + 32] + got_ref[: R + 32]
    share_ref[...] = jnp.broadcast_to(both[None], share_ref.shape)
    first = lax.rem(lax.axis_index("dp"), CORES) == 0
    mine, other = unpack(keep_ref[R + 32 :]), unpack(got_ref[R + 32 :])
    p_ref[:HALF] = jnp.where(first, mine, other)
    p_ref[HALF:] = jnp.where(first, other, mine)


def far_kernel(near_ref, share_ref):
    both = near_ref[0] + near_ref[1] + (near_ref[2] + near_ref[3])
    share_ref[...] = jnp.broadcast_to(both[None], share_ref.shape)


def splat_row(x, row):
    return jnp.broadcast_to(x[row : row + 1, :], (8, 128))


def inverse_factor(gram):
    rows = lax.broadcasted_iota(jnp.int32, (R, R), 0)
    eye = (rows == lax.broadcasted_iota(jnp.int32, (R, R), 1)).astype(F32)
    both = jnp.concatenate([gram, eye], 1)
    n = R // 8
    strips = [both[8 * t : 8 * t + 8] for t in range(n)]
    sub = lax.broadcasted_iota(jnp.int32, (8, 128), 0)
    scaled = []
    for s in range(n):
        cols = [
            [jnp.broadcast_to(strips[t][:, 8 * s + j : 8 * s + j + 1], (8, 128)) for t in range(s, n)]
            for j in range(8)
        ]
        done = jnp.zeros((8, 128), F32)
        for j in range(8):
            pivot, row = splat_row(cols[j][0], j), splat_row(strips[s], j)
            root = lax.rsqrt(pivot)
            root = root * (1.5 - 0.5 * pivot * root * root)
            done = jnp.where(sub == j, row * root, done)
            factors = [c * (root * root) for c in cols[j]]
            factors[0] = jnp.where(sub > j, factors[0], 0.0)
            for i in range(j + 1, 8):
                entry = splat_row(cols[i][0], j)
                cols[i] = [c - f * entry for c, f in zip(cols[i], factors)]
            for t in range(s, n):
                strips[t] = strips[t] - factors[t - s] * row
        scaled.append(done)
    return jnp.concatenate(scaled, 0)[:, R:]


def factor_kernel(far_ref, p_ref, q_ref, p_round_ref):
    both = far_ref[0] + far_ref[1] + (far_ref[2] + far_ref[3])
    inverse = inverse_factor(unpack(both[R:]))
    q = (dot(inverse, both[:R], ((1,), (0,)), precision=HIGH) * (1.0 / DP)).astype(BF16)
    q_ref[...] = jnp.broadcast_to(q[None], q_ref.shape)
    p_round_ref[...] = dot(p_ref[...], inverse, ((1,), (1,)), precision=HIGH).astype(BF16)


def update_kernel(
    q_ref, p_ref, rows_ref, update_ref, error_ref, q_new_ref, update_out, error_out, q_new_out, sems, q_sem
):
    width = D // PARTS
    z = lax.axis_index("tensor")
    for c in range(CORES):
        q_new_out[:, 128 * c : 128 * (c + 1)] = q_ref[CORES * z + c].astype(F32)
    q_copy = pltpu.make_async_copy(q_new_out, q_new_ref, q_sem)
    q_copy.start()

    def copies(n):
        span = pl.ds(n * width, width)
        return [
            pltpu.make_async_copy(update_out.at[:, span], update_ref.at[:, span], sems.at[0, n]),
            pltpu.make_async_copy(error_out.at[:, span], error_ref.at[0, :, span], sems.at[1, n]),
        ]

    for n in range(PARTS):
        for k in range(n * width // COLS, (n + 1) * width // COLS):
            q = jnp.concatenate([q_ref[CORES * k + c] for c in range(CORES)], 1)
            full = dot(p_ref[...], q, ((1,), (0,)))
            span = slice(COLS * k, COLS * (k + 1))
            update_out[:, span] = full.astype(BF16)
            error_out[:, span] = (rows_ref[:, span].astype(F32) - full).astype(BF16)
        for copy in copies(n):
            copy.start()
    for n in range(PARTS):
        for copy in copies(n):
            copy.wait()
    q_copy.wait()


def kernel_call(kernel, mib=4, **kw):
    return pl.pallas_call(
        kernel, compiler_params=pltpu.CompilerParams(vmem_limit_bytes=mib << 20), **kw
    )


def body(grad, error, q_start):
    vmem, hbm = pl.BlockSpec(memory_space=pltpu.VMEM), pl.BlockSpec(memory_space=pltpu.HBM)
    factor_t = lax.ppermute(q_start.T, ("dp", "tensor"), factor_route())
    corrected = (grad[0].astype(F32) + error[0].astype(F32)).astype(BF16)
    blocks = kernel_call(block_kernel, out_shape=shape(DP, HALF, COLS, dtype=BF16))(corrected)
    blocks = lax.all_to_all(blocks, "dp", 0, 0)
    total, part = kernel_call(
        sketch_kernel, out_shape=(shape(HALF, COLS), shape(CHIPS, 32, 128))
    )(blocks, factor_t)
    part = lax.all_to_all(part, "dp", 0, 0, axis_index_groups=PLANE)
    give, keep = kernel_call(basis_kernel, out_shape=(shape(128, 128), shape(128, 128)))(part, total)
    got = lax.ppermute(give, "dp", SWAP)
    near, p_sum = kernel_call(near_kernel, out_shape=(shape(4, R + 32, 128), shape(ROWS, R)))(keep, got)
    near = lax.all_to_all(near, "tensor", 0, 0, axis_index_groups=NEAR)
    far = kernel_call(far_kernel, out_shape=shape(4, R + 32, 128))(near)
    far = lax.all_to_all(far, "tensor", 0, 0, axis_index_groups=FAR)
    q_blocks, p_round = kernel_call(
        factor_kernel,
        out_shape=(shape(DP, R, 128, dtype=BF16), shape(ROWS, R, dtype=BF16)),
    )(far, p_sum)
    q_blocks = lax.all_to_all(q_blocks, "dp", 0, 0)
    update, new_error, q_mine = kernel_call(
        update_kernel,
        in_specs=[vmem, vmem, vmem],
        out_specs=[hbm, hbm, hbm],
        out_shape=(shape(ROWS, D, dtype=BF16), shape(1, ROWS, D, dtype=BF16), shape(R, COLS)),
        scratch_shapes=[
            pltpu.VMEM((ROWS, D), BF16),
            pltpu.VMEM((ROWS, D), BF16),
            pltpu.VMEM((R, COLS), F32),
            pltpu.SemaphoreType.DMA((2, PARTS)),
            pltpu.SemaphoreType.DMA,
        ],
    )(q_blocks, p_round, corrected)
    return (update, new_error, q_mine.T)


def solution(mesh):
    placed = (P("dp", "tensor", None), P("dp", "tensor", None), P("tensor", None))
    return jax.shard_map(
        body,
        mesh=mesh,
        in_specs=placed,
        out_specs=(P("tensor", None), P("dp", "tensor", None), P("tensor", None)),
        check_vma=False,
    )
```

```python
import jax
import jax.numpy as jnp
from jax import lax
from jax.experimental import pallas as pl
from jax.experimental.pallas import tpu as pltpu
from jax.sharding import PartitionSpec as P

SIDE = 4
CHIPS = SIDE * SIDE
CORES = 2
DP = CHIPS * CORES
DEPTH = 16
ROWS = 128
HALF = ROWS // CORES
D = 4096
COLS = D // CHIPS
R = 64
PARTS = 4
HIGH = lax.Precision.HIGHEST
F32, BF16 = jnp.float32, jnp.bfloat16

PLANE = [[core + CORES * chip for chip in range(CHIPS)] for core in range(CORES)]
NEAR = [[4 * a + b for b in range(4)] for a in range(4)]
FAR = [[4 * a + b for a in range(4)] for b in range(4)]
SWAP = [(i, i ^ 1) for i in range(DP)]


def ring(a, b, n):
    return min((a - b) % n, (b - a) % n)


def factor_route():
    pairs = []
    for k in range(CHIPS):
        planes = sorted(range(DEPTH), key=lambda z: -ring(z, k, DEPTH))
        chips = sorted(
            range(CHIPS),
            key=lambda j: ring(j // SIDE, k // SIDE, SIDE) + ring(j % SIDE, k % SIDE, SIDE),
        )
        for z, j in zip(planes, chips):
            for core in range(CORES):
                pairs.append(((CORES * j + core) * DEPTH + k, (CORES * k + core) * DEPTH + z))
    return pairs


def shape(*dims, dtype=F32):
    return jax.ShapeDtypeStruct(dims, dtype)


def pack(x):
    return jnp.concatenate([x[:32, :R], x[32:, :R]], 1)


def unpack(x):
    return jnp.concatenate([x[:, :R], x[:, R:]], 0)


def dot(a, b, over, **kw):
    return lax.dot_general(a, b, (over, ((), ())), preferred_element_type=F32, **kw)


def block_kernel(rows_ref, out_ref):
    for k in range(CHIPS):
        for c in range(CORES):
            out_ref[CORES * k + c] = rows_ref[HALF * c : HALF * (c + 1), COLS * k : COLS * (k + 1)]


def sketch_kernel(blocks_ref, factor_ref, total_ref, share_ref):
    total = blocks_ref[0].astype(F32)
    for i in range(1, DP):
        total = total + blocks_ref[i].astype(F32)
    total_ref[...] = total
    part = pack(dot(total, factor_ref[...].astype(F32), ((1,), (1,)), precision=HIGH))
    share_ref[...] = jnp.broadcast_to(part[None], share_ref.shape)


def basis_kernel(share_ref, total_ref, give_ref, keep_ref):
    packed = share_ref[0]
    for k in range(1, CHIPS):
        packed = packed + share_ref[k]
    p = unpack(packed)
    first = lax.rem(lax.axis_index("dp"), CORES) == 0
    left = dot(p, total_ref[:, :128], ((0,), (0,)), precision=HIGH)
    right = dot(p, total_ref[:, 128:], ((0,), (0,)), precision=HIGH)
    gram = pack(dot(p, p, ((0,), (0,)), precision=HIGH))
    keep_ref[:R] = jnp.where(first, left, right)
    give_ref[:R] = jnp.where(first, right, left)
    for ref in (keep_ref, give_ref):
        ref[R : R + 32] = gram
        ref[R + 32 :] = packed


def near_kernel(keep_ref, got_ref, share_ref, p_ref):
    both = keep_ref[: R + 32] + got_ref[: R + 32]
    share_ref[...] = jnp.broadcast_to(both[None], share_ref.shape)
    first = lax.rem(lax.axis_index("dp"), CORES) == 0
    mine, other = unpack(keep_ref[R + 32 :]), unpack(got_ref[R + 32 :])
    p_ref[:HALF] = jnp.where(first, mine, other)
    p_ref[HALF:] = jnp.where(first, other, mine)


def far_kernel(near_ref, share_ref):
    share_ref[...] = near_ref[0] + near_ref[1] + (near_ref[2] + near_ref[3])


def splat_row(x, row):
    return jnp.broadcast_to(x[row : row + 1, :], (8, 128))


def inverse_factor(gram):
    rows = lax.broadcasted_iota(jnp.int32, (R, R), 0)
    eye = (rows == lax.broadcasted_iota(jnp.int32, (R, R), 1)).astype(F32)
    both = jnp.concatenate([gram, eye], 1)
    n = R // 8
    strips = [both[8 * t : 8 * t + 8] for t in range(n)]
    sub = lax.broadcasted_iota(jnp.int32, (8, 128), 0)
    scaled = []
    for s in range(n):
        cols = [
            [jnp.broadcast_to(strips[t][:, 8 * s + j : 8 * s + j + 1], (8, 128)) for t in range(s, n)]
            for j in range(8)
        ]
        done = jnp.zeros((8, 128), F32)
        for j in range(8):
            pivot, row = splat_row(cols[j][0], j), splat_row(strips[s], j)
            root = lax.rsqrt(pivot)
            root = root * (1.5 - 0.5 * pivot * root * root)
            done = jnp.where(sub == j, row * root, done)
            factors = [c * (root * root) for c in cols[j]]
            factors[0] = jnp.where(sub > j, factors[0], 0.0)
            for i in range(j + 1, 8):
                entry = splat_row(cols[i][0], j)
                cols[i] = [c - f * entry for c, f in zip(cols[i], factors)]
            for t in range(s, n):
                strips[t] = strips[t] - factors[t - s] * row
        scaled.append(done)
    return jnp.concatenate(scaled, 0)[:, R:]


def factor_kernel(far_ref, p_ref, q_ref, p_round_ref):
    both = far_ref[0] + far_ref[1] + (far_ref[2] + far_ref[3])
    inverse = inverse_factor(unpack(both[R:]))
    q = (dot(inverse, both[:R], ((1,), (0,)), precision=HIGH) * (1.0 / DP)).astype(BF16)
    q_ref[...] = jnp.broadcast_to(q[None], q_ref.shape)
    p_round_ref[...] = dot(p_ref[...], inverse, ((1,), (1,)), precision=HIGH).astype(BF16)


def update_kernel(
    q_ref, p_ref, rows_ref, update_ref, error_ref, q_new_ref, update_out, error_out, q_new_out, sems, q_sem
):
    width = D // PARTS
    z = lax.axis_index("tensor")
    for c in range(CORES):
        q_new_out[:, 128 * c : 128 * (c + 1)] = q_ref[CORES * z + c].astype(F32)
    q_copy = pltpu.make_async_copy(q_new_out, q_new_ref, q_sem)
    q_copy.start()

    def copies(n):
        span = pl.ds(n * width, width)
        return [
            pltpu.make_async_copy(update_out.at[:, span], update_ref.at[:, span], sems.at[0, n]),
            pltpu.make_async_copy(error_out.at[:, span], error_ref.at[0, :, span], sems.at[1, n]),
        ]

    for n in range(PARTS):
        for k in range(n * width // COLS, (n + 1) * width // COLS):
            q = jnp.concatenate([q_ref[CORES * k + c] for c in range(CORES)], 1)
            full = dot(p_ref[...], q, ((1,), (0,)))
            span = slice(COLS * k, COLS * (k + 1))
            update_out[:, span] = full.astype(BF16)
            error_out[:, span] = (rows_ref[:, span].astype(F32) - full).astype(BF16)
        for copy in copies(n):
            copy.start()
    for n in range(PARTS):
        for copy in copies(n):
            copy.wait()
    q_copy.wait()


def kernel_call(kernel, mib=4, **kw):
    return pl.pallas_call(
        kernel, compiler_params=pltpu.CompilerParams(vmem_limit_bytes=mib << 20), **kw
    )


def body(grad, error, q_start):
    vmem, hbm = pl.BlockSpec(memory_space=pltpu.VMEM), pl.BlockSpec(memory_space=pltpu.HBM)
    factor_t = lax.ppermute(q_start.T, ("dp", "tensor"), factor_route())
    corrected = (grad[0].astype(F32) + error[0].astype(F32)).astype(BF16)
    blocks = kernel_call(block_kernel, out_shape=shape(DP, HALF, COLS, dtype=BF16))(corrected)
    blocks = lax.all_to_all(blocks, "dp", 0, 0)
    total, part = kernel_call(
        sketch_kernel, out_shape=(shape(HALF, COLS), shape(CHIPS, 32, 128))
    )(blocks, factor_t)
    part = lax.all_to_all(part, "dp", 0, 0, axis_index_groups=PLANE)
    give, keep = kernel_call(basis_kernel, out_shape=(shape(128, 128), shape(128, 128)))(part, total)
    got = lax.ppermute(give, "dp", SWAP)
    near, p_sum = kernel_call(near_kernel, out_shape=(shape(4, R + 32, 128), shape(ROWS, R)))(keep, got)
    near = lax.all_to_all(near, "tensor", 0, 0, axis_index_groups=NEAR)
    far = kernel_call(far_kernel, out_shape=shape(R + 32, 128))(near)
    far = lax.all_gather(far, "tensor", axis_index_groups=FAR)
    q_blocks, p_round = kernel_call(
        factor_kernel,
        out_shape=(shape(DP, R, 128, dtype=BF16), shape(ROWS, R, dtype=BF16)),
    )(far, p_sum)
    q_blocks = lax.all_to_all(q_blocks, "dp", 0, 0)
    update, new_error, q_mine = kernel_call(
        update_kernel,
        in_specs=[vmem, vmem, vmem],
        out_specs=[hbm, hbm, hbm],
        out_shape=(shape(ROWS, D, dtype=BF16), shape(1, ROWS, D, dtype=BF16), shape(R, COLS)),
        scratch_shapes=[
            pltpu.VMEM((ROWS, D), BF16),
            pltpu.VMEM((ROWS, D), BF16),
            pltpu.VMEM((R, COLS), F32),
            pltpu.SemaphoreType.DMA((2, PARTS)),
            pltpu.SemaphoreType.DMA,
        ],
    )(q_blocks, p_round, corrected)
    return (update, new_error, q_mine.T)


def solution(mesh):
    placed = (P("dp", "tensor", None), P("dp", "tensor", None), P("tensor", None))
    return jax.shard_map(
        body,
        mesh=mesh,
        in_specs=placed,
        out_specs=(P("tensor", None), P("dp", "tensor", None), P("tensor", None)),
        check_vma=False,
    )
```

```python
import jax
import jax.numpy as jnp
from jax import lax
from jax.experimental import pallas as pl
from jax.experimental.pallas import tpu as pltpu
from jax.sharding import PartitionSpec as P

SIDE = 4
CHIPS = SIDE * SIDE
CORES = 2
DP = CHIPS * CORES
DEPTH = 16
ROWS = 128
HALF = ROWS // CORES
D = 4096
COLS = D // CHIPS
R = 64
PARTS = 4
HIGH = lax.Precision.HIGHEST
F32, BF16 = jnp.float32, jnp.bfloat16

PLANE = [[core + CORES * chip for chip in range(CHIPS)] for core in range(CORES)]
NEAR = [[4 * a + b for b in range(4)] for a in range(4)]
FAR = [[4 * a + b for a in range(4)] for b in range(4)]
SWAP = [(i, i ^ 1) for i in range(DP)]
PAIRED = [
    [(CORES * k + core) * DEPTH + 2 * a + b for b in range(2) for k in range(CHIPS)]
    for a in range(DEPTH // 2)
    for core in range(CORES)
]


def ring(a, b, n):
    return min((a - b) % n, (b - a) % n)


def factor_route():
    pairs = []
    for k in range(CHIPS):
        planes = sorted(range(DEPTH), key=lambda z: -ring(z, k, DEPTH))
        chips = sorted(
            range(CHIPS),
            key=lambda j: ring(j // SIDE, k // SIDE, SIDE) + ring(j % SIDE, k % SIDE, SIDE),
        )
        for z, j in zip(planes, chips):
            for core in range(CORES):
                pairs.append(((CORES * j + core) * DEPTH + k, (CORES * k + core) * DEPTH + z))
    return pairs


def shape(*dims, dtype=F32):
    return jax.ShapeDtypeStruct(dims, dtype)


def pack(x):
    return jnp.concatenate([x[:32, :R], x[32:, :R]], 1)


def unpack(x):
    return jnp.concatenate([x[:, :R], x[:, R:]], 0)


def dot(a, b, over, **kw):
    return lax.dot_general(a, b, (over, ((), ())), preferred_element_type=F32, **kw)


def block_kernel(rows_ref, out_ref):
    for k in range(CHIPS):
        for c in range(CORES):
            out_ref[CORES * k + c] = rows_ref[HALF * c : HALF * (c + 1), COLS * k : COLS * (k + 1)]


def sketch_kernel(blocks_ref, factor_ref, total_ref, share_ref):
    total = blocks_ref[0].astype(F32)
    for i in range(1, DP):
        total = total + blocks_ref[i].astype(F32)
    total_ref[...] = total
    part = pack(dot(total, factor_ref[...].astype(F32), ((1,), (1,)), precision=HIGH))
    share_ref[...] = jnp.broadcast_to(part[None], share_ref.shape)


def basis_kernel(share_ref, total_ref, give_ref, keep_ref):
    packed = share_ref[0]
    for k in range(1, CHIPS):
        packed = packed + share_ref[k]
    p = unpack(packed)
    first = lax.rem(lax.axis_index("dp"), CORES) == 0
    left = dot(p, total_ref[:, :128], ((0,), (0,)), precision=HIGH)
    right = dot(p, total_ref[:, 128:], ((0,), (0,)), precision=HIGH)
    gram = pack(dot(p, p, ((0,), (0,)), precision=HIGH))
    keep_ref[:R] = jnp.where(first, left, right)
    give_ref[:R] = jnp.where(first, right, left)
    for ref in (keep_ref, give_ref):
        ref[R : R + 32] = gram
        ref[R + 32 :] = packed


def near_kernel(keep_ref, got_ref, share_ref, p_ref):
    both = keep_ref[:R] + got_ref[:R]
    gram = keep_ref[R : R + 32] + got_ref[R : R + 32]
    for half in range(2):
        part = pack(both[:, R * half : R * (half + 1)])
        for m in (half, half + 2):
            share_ref[m, :32] = part
            share_ref[m, 32:] = gram
    first = lax.rem(lax.axis_index("dp"), CORES) == 0
    mine, other = unpack(keep_ref[R + 32 :]), unpack(got_ref[R + 32 :])
    p_ref[:HALF] = jnp.where(first, mine, other)
    p_ref[HALF:] = jnp.where(first, other, mine)


def far_kernel(near_ref, share_ref):
    share_ref[...] = near_ref[0] + near_ref[1] + (near_ref[2] + near_ref[3])


def splat_row(x, row):
    return jnp.broadcast_to(x[row : row + 1, :], (8, 128))


def inverse_factor(gram):
    rows = lax.broadcasted_iota(jnp.int32, (R, R), 0)
    eye = (rows == lax.broadcasted_iota(jnp.int32, (R, R), 1)).astype(F32)
    both = jnp.concatenate([gram, eye], 1)
    n = R // 8
    strips = [both[8 * t : 8 * t + 8] for t in range(n)]
    sub = lax.broadcasted_iota(jnp.int32, (8, 128), 0)
    scaled = []
    for s in range(n):
        cols = [
            [jnp.broadcast_to(strips[t][:, 8 * s + j : 8 * s + j + 1], (8, 128)) for t in range(s, n)]
            for j in range(8)
        ]
        done = jnp.zeros((8, 128), F32)
        for j in range(8):
            pivot, row = splat_row(cols[j][0], j), splat_row(strips[s], j)
            root = lax.rsqrt(pivot)
            done = jnp.where(sub == j, row * root, done)
            factors = [c * (root * root) for c in cols[j]]
            factors[0] = jnp.where(sub > j, factors[0], 0.0)
            for i in range(j + 1, 8):
                entry = splat_row(cols[i][0], j)
                cols[i] = [c - f * entry for c, f in zip(cols[i], factors)]
            for t in range(s, n):
                strips[t] = strips[t] - factors[t - s] * row
        scaled.append(done)
    return jnp.concatenate(scaled, 0)[:, R:]


def factor_kernel(far_ref, p_ref, q_ref, p_round_ref):
    both = far_ref[0] + far_ref[1] + (far_ref[2] + far_ref[3])
    inverse = inverse_factor(unpack(both[32:]))
    q_half = dot(inverse, unpack(both[:32]), ((1,), (0,)), precision=HIGH) * (1.0 / DP)
    q_ref[...] = jnp.broadcast_to(pack(q_half).astype(BF16)[None], q_ref.shape)
    p_round_ref[...] = dot(p_ref[...], inverse, ((1,), (1,)), precision=HIGH).astype(BF16)


def update_kernel(
    mine_ref, other_ref, p_ref, rows_ref, update_ref, error_ref, q_new_ref, update_out, error_out, q_new_out, sems, q_sem
):
    width = D // PARTS
    z = lax.axis_index("tensor")
    first = lax.rem(lax.axis_index("dp"), CORES) == 0

    def block(k, c):
        even, odd = (
            jnp.where(first if c == 0 else ~first, mine_ref[n + k].astype(F32), other_ref[n + k].astype(F32))
            for n in (0, CHIPS)
        )
        upper = jnp.concatenate([even[:, :R], odd[:, :R]], 1)
        lower = jnp.concatenate([even[:, R:], odd[:, R:]], 1)
        return jnp.concatenate([upper, lower], 0)

    for c in range(CORES):
        q_new_out[:, 128 * c : 128 * (c + 1)] = block(z, c)
    q_copy = pltpu.make_async_copy(q_new_out, q_new_ref, q_sem)
    q_copy.start()

    def copies(n):
        span = pl.ds(n * width, width)
        return [
            pltpu.make_async_copy(update_out.at[:, span], update_ref.at[:, span], sems.at[0, n]),
            pltpu.make_async_copy(error_out.at[:, span], error_ref.at[0, :, span], sems.at[1, n]),
        ]

    for n in range(PARTS):
        for k in range(n * width // COLS, (n + 1) * width // COLS):
            q = jnp.concatenate([block(k, c) for c in range(CORES)], 1).astype(BF16)
            full = dot(p_ref[...], q, ((1,), (0,)))
            span = slice(COLS * k, COLS * (k + 1))
            update_out[:, span] = full.astype(BF16)
            error_out[:, span] = (rows_ref[:, span].astype(F32) - full).astype(BF16)
        for copy in copies(n):
            copy.start()
    for n in range(PARTS):
        for copy in copies(n):
            copy.wait()
    q_copy.wait()


def kernel_call(kernel, mib=4, **kw):
    return pl.pallas_call(
        kernel, compiler_params=pltpu.CompilerParams(vmem_limit_bytes=mib << 20), **kw
    )


def body(grad, error, q_start):
    vmem, hbm = pl.BlockSpec(memory_space=pltpu.VMEM), pl.BlockSpec(memory_space=pltpu.HBM)
    factor_t = lax.ppermute(q_start.T, ("dp", "tensor"), factor_route())
    corrected = (grad[0].astype(F32) + error[0].astype(F32)).astype(BF16)
    blocks = kernel_call(block_kernel, out_shape=shape(DP, HALF, COLS, dtype=BF16))(corrected)
    blocks = lax.all_to_all(blocks, "dp", 0, 0)
    total, part = kernel_call(
        sketch_kernel, out_shape=(shape(HALF, COLS), shape(CHIPS, 32, 128))
    )(blocks, factor_t)
    part = lax.all_to_all(part, "dp", 0, 0, axis_index_groups=PLANE)
    give, keep = kernel_call(basis_kernel, out_shape=(shape(128, 128), shape(128, 128)))(part, total)
    got = lax.ppermute(give, "dp", SWAP)
    near, p_sum = kernel_call(near_kernel, out_shape=(shape(4, 64, 128), shape(ROWS, R)))(keep, got)
    near = lax.all_to_all(near, "tensor", 0, 0, axis_index_groups=NEAR)
    far = kernel_call(far_kernel, out_shape=shape(64, 128))(near)
    far = lax.all_gather(far, "tensor", axis_index_groups=FAR)
    q_blocks, p_round = kernel_call(
        factor_kernel,
        out_shape=(shape(2 * CHIPS, 32, 128, dtype=BF16), shape(ROWS, R, dtype=BF16)),
    )(far, p_sum)
    q_mine = lax.all_to_all(q_blocks, ("dp", "tensor"), 0, 0, axis_index_groups=PAIRED)
    q_other = lax.ppermute(q_mine, "dp", SWAP)
    update, new_error, q_new = kernel_call(
        update_kernel,
        in_specs=[vmem, vmem, vmem, vmem],
        out_specs=[hbm, hbm, hbm],
        out_shape=(shape(ROWS, D, dtype=BF16), shape(1, ROWS, D, dtype=BF16), shape(R, COLS)),
        scratch_shapes=[
            pltpu.VMEM((ROWS, D), BF16),
            pltpu.VMEM((ROWS, D), BF16),
            pltpu.VMEM((R, COLS), F32),
            pltpu.SemaphoreType.DMA((2, PARTS)),
            pltpu.SemaphoreType.DMA,
        ],
    )(q_mine, q_other, p_round, corrected)
    return (update, new_error, q_new.T)


def solution(mesh):
    placed = (P("dp", "tensor", None), P("dp", "tensor", None), P("tensor", None))
    return jax.shard_map(
        body,
        mesh=mesh,
        in_specs=placed,
        out_specs=(P("tensor", None), P("dp", "tensor", None), P("tensor", None)),
        check_vma=False,
    )
```

```python
import jax
import jax.numpy as jnp
from jax import lax
from jax.experimental import pallas as pl
from jax.experimental.pallas import tpu as pltpu
from jax.sharding import PartitionSpec as P

SIDE = 4
CHIPS = SIDE * SIDE
CORES = 2
DP = CHIPS * CORES
DEPTH = 16
ROWS = 128
HALF = ROWS // CORES
D = 4096
COLS = D // CHIPS
R = 64
GRAM = 24
PARTS = 4
HIGH = lax.Precision.HIGHEST
F32, BF16 = jnp.float32, jnp.bfloat16

PLANE = [[core + CORES * chip for chip in range(CHIPS)] for core in range(CORES)]
NEAR = [[4 * a + b for b in range(4)] for a in range(4)]
FAR = [[4 * a + b for a in range(4)] for b in range(4)]
SWAP = [(i, i ^ 1) for i in range(DP)]
PAIRED = [
    [(CORES * k + core) * DEPTH + 2 * a + b for b in range(2) for k in range(CHIPS)]
    for a in range(DEPTH // 2)
    for core in range(CORES)
]


def ring(a, b, n):
    return min((a - b) % n, (b - a) % n)


def factor_route():
    pairs = []
    for k in range(CHIPS):
        planes = sorted(range(DEPTH), key=lambda z: -ring(z, k, DEPTH))
        chips = sorted(
            range(CHIPS),
            key=lambda j: ring(j // SIDE, k // SIDE, SIDE) + ring(j % SIDE, k % SIDE, SIDE),
        )
        for z, j in zip(planes, chips):
            for core in range(CORES):
                pairs.append(((CORES * j + core) * DEPTH + k, (CORES * k + core) * DEPTH + z))
    return pairs


def shape(*dims, dtype=F32):
    return jax.ShapeDtypeStruct(dims, dtype)


def pack(x):
    return jnp.concatenate([x[:32, :R], x[32:, :R]], 1)


def fold(gram):
    corners = (gram[:32, :32], gram[:32, 32:], gram[32:, 32:])
    return jnp.concatenate(
        [jnp.concatenate([x[8 * n : 8 * n + 8] for n in range(4)], 1) for x in corners], 0
    )


def unfold(x):
    a, b, c = (
        jnp.concatenate([x[8 * m : 8 * m + 8, 32 * n : 32 * n + 32] for n in range(4)], 0)
        for m in range(3)
    )
    upper = jnp.concatenate([jnp.concatenate([a, b], 1), jnp.concatenate([jnp.zeros_like(b), c], 1)], 0)
    rows = lax.broadcasted_iota(jnp.int32, (R, R), 0)
    return jnp.where((rows >= 32) & (lax.broadcasted_iota(jnp.int32, (R, R), 1) < 32), upper.T, upper)


def unpack(x):
    return jnp.concatenate([x[:, :R], x[:, R:]], 0)


def dot(a, b, over, **kw):
    return lax.dot_general(a, b, (over, ((), ())), preferred_element_type=F32, **kw)


def block_kernel(grad_ref, error_ref, out_ref, grad_in, error_in, blocks, in_sems, out_sems):
    size = ROWS // PARTS

    def arrivals(n):
        rows = pl.ds(n * size, size)
        return [
            pltpu.make_async_copy(grad_ref.at[0, rows], grad_in.at[rows], in_sems.at[0, n]),
            pltpu.make_async_copy(error_ref.at[0, rows], error_in.at[rows], in_sems.at[1, n]),
        ]

    def departure(c):
        return pltpu.make_async_copy(blocks.at[:, c], out_ref.at[:, c], out_sems.at[c])

    for n in range(PARTS):
        for copy in arrivals(n):
            copy.start()
    for n in range(PARTS):
        for copy in arrivals(n):
            copy.wait()
        c, row = divmod(n * size, HALF)
        rows = slice(n * size, (n + 1) * size)
        for k in range(CHIPS):
            span = slice(COLS * k, COLS * (k + 1))
            x = grad_in[rows, span].astype(F32) + error_in[rows, span].astype(F32)
            blocks[k, c, row : row + size] = x.astype(BF16)
        if row + size == HALF:
            departure(c).start()
    for c in range(CORES):
        departure(c).wait()


def sketch_kernel(blocks_ref, factor_ref, total_ref, share_ref):
    total = blocks_ref[0].astype(F32)
    for i in range(1, DP):
        total = total + blocks_ref[i].astype(F32)
    total_ref[...] = total
    part = pack(dot(total, factor_ref[...].astype(F32), ((1,), (1,)), precision=HIGH))
    share_ref[...] = jnp.broadcast_to(part[None], share_ref.shape)


def basis_kernel(share_ref, total_ref, give_ref, keep_ref):
    packed = share_ref[0]
    for k in range(1, CHIPS):
        packed = packed + share_ref[k]
    p = unpack(packed)
    first = lax.rem(lax.axis_index("dp"), CORES) == 0
    left = dot(p, total_ref[:, :128], ((0,), (0,)), precision=HIGH)
    right = dot(p, total_ref[:, 128:], ((0,), (0,)), precision=HIGH)
    gram = fold(dot(p, p, ((0,), (0,)), precision=HIGH))
    keep_ref[:R] = jnp.where(first, left, right)
    give_ref[:R] = jnp.where(first, right, left)
    for ref in (keep_ref, give_ref):
        ref[R : R + GRAM] = gram
        ref[R + GRAM :] = packed


def near_kernel(keep_ref, got_ref, share_ref, p_ref):
    both = keep_ref[:R] + got_ref[:R]
    gram = keep_ref[R : R + GRAM] + got_ref[R : R + GRAM]
    for half in range(2):
        part = pack(both[:, R * half : R * (half + 1)])
        for m in (half, half + 2):
            share_ref[m, :32] = part
            share_ref[m, 32:] = gram
    first = lax.rem(lax.axis_index("dp"), CORES) == 0
    mine, other = unpack(keep_ref[R + GRAM :]), unpack(got_ref[R + GRAM :])
    p_ref[:HALF] = jnp.where(first, mine, other)
    p_ref[HALF:] = jnp.where(first, other, mine)


def far_kernel(near_ref, share_ref):
    share_ref[...] = near_ref[0] + near_ref[1] + (near_ref[2] + near_ref[3])


def splat_row(x, row):
    return jnp.broadcast_to(x[row : row + 1, :], (8, 128))


def inverse_factor(gram):
    rows = lax.broadcasted_iota(jnp.int32, (R, R), 0)
    eye = (rows == lax.broadcasted_iota(jnp.int32, (R, R), 1)).astype(F32)
    both = jnp.concatenate([gram, eye], 1)
    n = R // 8
    strips = [both[8 * t : 8 * t + 8] for t in range(n)]
    sub = lax.broadcasted_iota(jnp.int32, (8, 128), 0)
    scaled = []
    for s in range(n):
        cols = [
            [jnp.broadcast_to(strips[t][:, 8 * s + j : 8 * s + j + 1], (8, 128)) for t in range(s, n)]
            for j in range(8)
        ]
        done = jnp.zeros((8, 128), F32)
        for j in range(8):
            pivot, row = splat_row(cols[j][0], j), splat_row(strips[s], j)
            root = lax.rsqrt(pivot)
            done = jnp.where(sub == j, row * root, done)
            factors = [c * (root * root) for c in cols[j]]
            factors[0] = jnp.where(sub > j, factors[0], 0.0)
            for i in range(j + 1, 8):
                entry = splat_row(cols[i][0], j)
                cols[i] = [c - f * entry for c, f in zip(cols[i], factors)]
            for t in range(s, n):
                strips[t] = strips[t] - factors[t - s] * row
        scaled.append(done)
    return jnp.concatenate(scaled, 0)[:, R:]


def factor_kernel(far_ref, p_ref, q_ref, p_round_ref):
    both = far_ref[0] + far_ref[1] + (far_ref[2] + far_ref[3])
    inverse = inverse_factor(unfold(both[32:]))
    q_half = dot(inverse, unpack(both[:32]), ((1,), (0,)), precision=HIGH) * (1.0 / DP)
    q_ref[...] = jnp.broadcast_to(pack(q_half).astype(BF16)[None], q_ref.shape)
    p_round_ref[...] = dot(p_ref[...], inverse, ((1,), (1,)), precision=HIGH).astype(BF16)


def update_kernel(
    mine_ref, other_ref, p_ref, rows_ref, update_ref, error_ref, q_new_ref, update_out, error_out, q_new_out, sems, q_sem
):
    width = D // PARTS
    z = lax.axis_index("tensor")
    first = lax.rem(lax.axis_index("dp"), CORES) == 0

    def block(k, c):
        even, odd = (
            jnp.where(first if c == 0 else ~first, mine_ref[n + k], other_ref[n + k])
            for n in (0, CHIPS)
        )
        upper = jnp.concatenate([even[:, :R], odd[:, :R]], 1)
        lower = jnp.concatenate([even[:, R:], odd[:, R:]], 1)
        return jnp.concatenate([upper, lower], 0)

    for c in range(CORES):
        q_new_out[:, 128 * c : 128 * (c + 1)] = block(z, c).astype(F32)
    q_copy = pltpu.make_async_copy(q_new_out, q_new_ref, q_sem)
    q_copy.start()

    def copies(n):
        span = pl.ds(n * width, width)
        return [
            pltpu.make_async_copy(update_out.at[:, span], update_ref.at[:, span], sems.at[0, n]),
            pltpu.make_async_copy(error_out.at[:, span], error_ref.at[0, :, span], sems.at[1, n]),
        ]

    for n in range(PARTS):
        for k in range(n * width // COLS, (n + 1) * width // COLS):
            q = jnp.concatenate([block(k, c) for c in range(CORES)], 1)
            full = dot(p_ref[...], q, ((1,), (0,)))
            span = slice(COLS * k, COLS * (k + 1))
            update_out[:, span] = full.astype(BF16)
            error_out[:, span] = (rows_ref[:, span].astype(F32) - full).astype(BF16)
        for copy in copies(n):
            copy.start()
    for n in range(PARTS):
        for copy in copies(n):
            copy.wait()
    q_copy.wait()


def kernel_call(kernel, mib=4, **kw):
    return pl.pallas_call(
        kernel, compiler_params=pltpu.CompilerParams(vmem_limit_bytes=mib << 20), **kw
    )


def body(grad, error, q_start):
    vmem, hbm = pl.BlockSpec(memory_space=pltpu.VMEM), pl.BlockSpec(memory_space=pltpu.HBM)
    factor_t = lax.ppermute(q_start.T, ("dp", "tensor"), factor_route())
    corrected = (grad[0].astype(F32) + error[0].astype(F32)).astype(BF16)
    blocks = kernel_call(
        block_kernel,
        mib=56,
        in_specs=[hbm, hbm],
        out_specs=hbm,
        out_shape=shape(CHIPS, CORES, HALF, COLS, dtype=BF16),
        scratch_shapes=[
            pltpu.VMEM((ROWS, D), BF16),
            pltpu.VMEM((ROWS, D), BF16),
            pltpu.VMEM((CHIPS, CORES, HALF, COLS), BF16),
            pltpu.SemaphoreType.DMA((2, PARTS)),
            pltpu.SemaphoreType.DMA((CORES,)),
        ],
    )(grad, error)
    blocks = lax.all_to_all(blocks.reshape(DP, HALF, COLS), "dp", 0, 0)
    total, part = kernel_call(
        sketch_kernel, out_shape=(shape(HALF, COLS), shape(CHIPS, 32, 128))
    )(blocks, factor_t)
    part = lax.all_to_all(part, "dp", 0, 0, axis_index_groups=PLANE)
    give, keep = kernel_call(basis_kernel, out_shape=(shape(R + GRAM + 32, 128),) * 2)(part, total)
    got = lax.ppermute(give, "dp", SWAP)
    near, p_sum = kernel_call(near_kernel, out_shape=(shape(4, 32 + GRAM, 128), shape(ROWS, R)))(keep, got)
    near = lax.all_to_all(near, "tensor", 0, 0, axis_index_groups=NEAR)
    far = kernel_call(far_kernel, out_shape=shape(32 + GRAM, 128))(near)
    far = lax.all_gather(far, "tensor", axis_index_groups=FAR)
    q_blocks, p_round = kernel_call(
        factor_kernel,
        out_shape=(shape(2 * CHIPS, 32, 128, dtype=BF16), shape(ROWS, R, dtype=BF16)),
    )(far, p_sum)
    q_mine = lax.all_to_all(q_blocks, ("dp", "tensor"), 0, 0, axis_index_groups=PAIRED)
    q_other = lax.ppermute(q_mine, "dp", SWAP)
    update, new_error, q_new = kernel_call(
        update_kernel,
        in_specs=[vmem, vmem, vmem, vmem],
        out_specs=[hbm, hbm, hbm],
        out_shape=(shape(ROWS, D, dtype=BF16), shape(1, ROWS, D, dtype=BF16), shape(R, COLS)),
        scratch_shapes=[
            pltpu.VMEM((ROWS, D), BF16),
            pltpu.VMEM((ROWS, D), BF16),
            pltpu.VMEM((R, COLS), F32),
            pltpu.SemaphoreType.DMA((2, PARTS)),
            pltpu.SemaphoreType.DMA,
        ],
    )(q_mine, q_other, p_round, corrected)
    return (update, new_error, q_new.T)


def solution(mesh):
    placed = (P("dp", "tensor", None), P("dp", "tensor", None), P("tensor", None))
    return jax.shard_map(
        body,
        mesh=mesh,
        in_specs=placed,
        out_specs=(P("tensor", None), P("dp", "tensor", None), P("tensor", None)),
        check_vma=False,
    )
```

```python
import jax
import jax.numpy as jnp
from jax import lax
from jax.experimental import pallas as pl
from jax.experimental.pallas import tpu as pltpu
from jax.sharding import PartitionSpec as P

SIDE = 4
CHIPS = SIDE * SIDE
CORES = 2
DP = CHIPS * CORES
DEPTH = 16
ROWS = 128
HALF = ROWS // CORES
D = 4096
COLS = D // CHIPS
R = 64
GRAM = 24
PARTS = 4
HIGH = lax.Precision.HIGHEST
F32, BF16 = jnp.float32, jnp.bfloat16

PLANE = [[core + CORES * chip for chip in range(CHIPS)] for core in range(CORES)]
NEAR = [[4 * a + b for b in range(4)] for a in range(4)]
FAR = [[4 * a + b for a in range(4)] for b in range(4)]
SWAP = [(i, i ^ 1) for i in range(DP)]
PAIRED = [
    [(CORES * k + core) * DEPTH + 2 * a + b for b in range(2) for k in range(CHIPS)]
    for a in range(DEPTH // 2)
    for core in range(CORES)
]


def ring(a, b, n):
    return min((a - b) % n, (b - a) % n)


def factor_route():
    pairs = []
    for k in range(CHIPS):
        planes = sorted(range(DEPTH), key=lambda z: -ring(z, k, DEPTH))
        chips = sorted(
            range(CHIPS),
            key=lambda j: ring(j // SIDE, k // SIDE, SIDE) + ring(j % SIDE, k % SIDE, SIDE),
        )
        for z, j in zip(planes, chips):
            for core in range(CORES):
                pairs.append(((CORES * j + core) * DEPTH + k, (CORES * k + core) * DEPTH + z))
    return pairs


def shape(*dims, dtype=F32):
    return jax.ShapeDtypeStruct(dims, dtype)


def pack(x):
    return jnp.concatenate([x[:32, :R], x[32:, :R]], 1)


def fold(gram):
    corners = (gram[:32, :32], gram[:32, 32:], gram[32:, 32:])
    return jnp.concatenate(
        [jnp.concatenate([x[8 * n : 8 * n + 8] for n in range(4)], 1) for x in corners], 0
    )


def unfold(x):
    a, b, c = (
        jnp.concatenate([x[8 * m : 8 * m + 8, 32 * n : 32 * n + 32] for n in range(4)], 0)
        for m in range(3)
    )
    upper = jnp.concatenate([jnp.concatenate([a, b], 1), jnp.concatenate([jnp.zeros_like(b), c], 1)], 0)
    rows = lax.broadcasted_iota(jnp.int32, (R, R), 0)
    return jnp.where((rows >= 32) & (lax.broadcasted_iota(jnp.int32, (R, R), 1) < 32), upper.T, upper)


def unpack(x):
    return jnp.concatenate([x[:, :R], x[:, R:]], 0)


def dot(a, b, over, **kw):
    return lax.dot_general(a, b, (over, ((), ())), preferred_element_type=F32, **kw)


def block_kernel(grad_ref, error_ref, out_ref, grad_in, error_in, blocks, in_sems, out_sems):
    size = ROWS // PARTS

    def arrivals(n):
        rows = pl.ds(n * size, size)
        return [
            pltpu.make_async_copy(grad_ref.at[0, rows], grad_in.at[rows], in_sems.at[0, n]),
            pltpu.make_async_copy(error_ref.at[0, rows], error_in.at[rows], in_sems.at[1, n]),
        ]

    def departure(c):
        return pltpu.make_async_copy(blocks.at[:, c], out_ref.at[:, c], out_sems.at[c])

    for n in range(PARTS):
        for copy in arrivals(n):
            copy.start()
    for n in range(PARTS):
        for copy in arrivals(n):
            copy.wait()
        c, row = divmod(n * size, HALF)
        rows = slice(n * size, (n + 1) * size)
        for k in range(CHIPS):
            span = slice(COLS * k, COLS * (k + 1))
            x = grad_in[rows, span].astype(F32) + error_in[rows, span].astype(F32)
            blocks[k, c, row : row + size] = x.astype(BF16)
        if row + size == HALF:
            departure(c).start()
    for c in range(CORES):
        departure(c).wait()


def sketch_kernel(blocks_ref, factor_ref, total_ref, share_ref):
    total = blocks_ref[0].astype(F32)
    for i in range(1, DP):
        total = total + blocks_ref[i].astype(F32)
    total_ref[...] = total
    part = pack(dot(total, factor_ref[...].astype(F32), ((1,), (1,)), precision=HIGH))
    share_ref[...] = jnp.broadcast_to(part[None], share_ref.shape)


def basis_kernel(share_ref, total_ref, give_ref, keep_ref):
    packed = share_ref[0]
    for k in range(1, CHIPS):
        packed = packed + share_ref[k]
    p = unpack(packed)
    first = lax.rem(lax.axis_index("dp"), CORES) == 0
    left = dot(p, total_ref[:, :128], ((0,), (0,)), precision=HIGH)
    right = dot(p, total_ref[:, 128:], ((0,), (0,)), precision=HIGH)
    gram = fold(dot(p, p, ((0,), (0,)), precision=HIGH))
    keep_ref[:R] = jnp.where(first, left, right)
    give_ref[:R] = jnp.where(first, right, left)
    for ref in (keep_ref, give_ref):
        ref[R : R + GRAM] = gram
        ref[R + GRAM :] = packed


def near_kernel(keep_ref, got_ref, share_ref, p_ref):
    both = keep_ref[:R] + got_ref[:R]
    gram = keep_ref[R : R + GRAM] + got_ref[R : R + GRAM]
    for half in range(2):
        part = pack(both[:, R * half : R * (half + 1)])
        for m in (half, half + 2):
            share_ref[m, :32] = part
            share_ref[m, 32:] = gram
    first = lax.rem(lax.axis_index("dp"), CORES) == 0
    mine, other = unpack(keep_ref[R + GRAM :]), unpack(got_ref[R + GRAM :])
    p_ref[:HALF] = jnp.where(first, mine, other)
    p_ref[HALF:] = jnp.where(first, other, mine)


def far_kernel(near_ref, share_ref):
    share_ref[...] = near_ref[0] + near_ref[1] + (near_ref[2] + near_ref[3])


def splat_row(x, row):
    return jnp.broadcast_to(x[row : row + 1, :], (8, 128))


def inverse_factor(gram):
    rows = lax.broadcasted_iota(jnp.int32, (R, R), 0)
    eye = (rows == lax.broadcasted_iota(jnp.int32, (R, R), 1)).astype(F32)
    both = jnp.concatenate([gram, eye], 1)
    n = R // 8
    strips = [both[8 * t : 8 * t + 8] for t in range(n)]
    sub = lax.broadcasted_iota(jnp.int32, (8, 128), 0)
    scaled = []
    for s in range(n):
        cols = [
            [jnp.broadcast_to(strips[t][:, 8 * s + j : 8 * s + j + 1], (8, 128)) for t in range(s, n)]
            for j in range(8)
        ]
        done = jnp.zeros((8, 128), F32)
        for j in range(8):
            pivot, row = splat_row(cols[j][0], j), splat_row(strips[s], j)
            root = lax.rsqrt(pivot)
            done = jnp.where(sub == j, row * root, done)
            factors = [c * (root * root) for c in cols[j]]
            factors[0] = jnp.where(sub > j, factors[0], 0.0)
            for i in range(j + 1, 8):
                entry = splat_row(cols[i][0], j)
                cols[i] = [c - f * entry for c, f in zip(cols[i], factors)]
            for t in range(s, n):
                strips[t] = strips[t] - factors[t - s] * row
        scaled.append(done)
    return jnp.concatenate(scaled, 0)[:, R:]


def factor_kernel(far_ref, p_ref, q_ref, p_round_ref):
    both = far_ref[:, :128] + far_ref[:, 128:256] + (far_ref[:, 256:384] + far_ref[:, 384:])
    inverse = inverse_factor(unfold(both[32:]))
    q_half = dot(inverse, unpack(both[:32]), ((1,), (0,)), precision=HIGH) * (1.0 / DP)
    q_ref[...] = jnp.broadcast_to(pack(q_half).astype(BF16)[None], q_ref.shape)
    p_round_ref[...] = dot(p_ref[...], inverse, ((1,), (1,)), precision=HIGH).astype(BF16)


def update_kernel(
    mine_ref, other_ref, p_ref, rows_ref, update_ref, error_ref, q_new_ref, update_out, error_out, q_new_out, sems, q_sem
):
    width = D // PARTS
    z = lax.axis_index("tensor")
    first = lax.rem(lax.axis_index("dp"), CORES) == 0

    def block(k, c):
        even, odd = (
            jnp.where(first if c == 0 else ~first, mine_ref[n + k], other_ref[n + k])
            for n in (0, CHIPS)
        )
        upper = jnp.concatenate([even[:, :R], odd[:, :R]], 1)
        lower = jnp.concatenate([even[:, R:], odd[:, R:]], 1)
        return jnp.concatenate([upper, lower], 0)

    for c in range(CORES):
        q_new_out[:, 128 * c : 128 * (c + 1)] = block(z, c).astype(F32)
    q_copy = pltpu.make_async_copy(q_new_out, q_new_ref, q_sem)
    q_copy.start()

    def copies(n):
        span = pl.ds(n * width, width)
        return [
            pltpu.make_async_copy(update_out.at[:, span], update_ref.at[:, span], sems.at[0, n]),
            pltpu.make_async_copy(error_out.at[:, span], error_ref.at[0, :, span], sems.at[1, n]),
        ]

    for n in range(PARTS):
        for k in range(n * width // COLS, (n + 1) * width // COLS):
            q = jnp.concatenate([block(k, c) for c in range(CORES)], 1)
            full = dot(p_ref[...], q, ((1,), (0,)))
            span = slice(COLS * k, COLS * (k + 1))
            update_out[:, span] = full.astype(BF16)
            error_out[:, span] = (rows_ref[:, span].astype(F32) - full).astype(BF16)
        for copy in copies(n):
            copy.start()
    for n in range(PARTS):
        for copy in copies(n):
            copy.wait()
    q_copy.wait()


def kernel_call(kernel, mib=4, **kw):
    return pl.pallas_call(
        kernel, compiler_params=pltpu.CompilerParams(vmem_limit_bytes=mib << 20), **kw
    )


def body(grad, error, q_start):
    vmem, hbm = pl.BlockSpec(memory_space=pltpu.VMEM), pl.BlockSpec(memory_space=pltpu.HBM)
    factor_t = lax.ppermute(q_start.T, ("dp", "tensor"), factor_route())
    corrected = (grad[0].astype(F32) + error[0].astype(F32)).astype(BF16)
    blocks = kernel_call(
        block_kernel,
        mib=56,
        in_specs=[hbm, hbm],
        out_specs=hbm,
        out_shape=shape(CHIPS, CORES, HALF, COLS, dtype=BF16),
        scratch_shapes=[
            pltpu.VMEM((ROWS, D), BF16),
            pltpu.VMEM((ROWS, D), BF16),
            pltpu.VMEM((CHIPS, CORES, HALF, COLS), BF16),
            pltpu.SemaphoreType.DMA((2, PARTS)),
            pltpu.SemaphoreType.DMA((CORES,)),
        ],
    )(grad, error)
    blocks = lax.all_to_all(blocks.reshape(DP, HALF, COLS), "dp", 0, 0)
    total, part = kernel_call(
        sketch_kernel, out_shape=(shape(HALF, COLS), shape(CHIPS, 32, 128))
    )(blocks, factor_t)
    part = lax.all_to_all(part, "dp", 0, 0, axis_index_groups=PLANE)
    give, keep = kernel_call(basis_kernel, out_shape=(shape(R + GRAM + 32, 128),) * 2)(part, total)
    got = lax.ppermute(give, "dp", SWAP)
    near, p_sum = kernel_call(near_kernel, out_shape=(shape(4, 32 + GRAM, 128), shape(ROWS, R)))(keep, got)
    near = lax.all_to_all(near, "tensor", 0, 0, axis_index_groups=NEAR)
    far = kernel_call(far_kernel, out_shape=shape(32 + GRAM, 128))(near)
    far = lax.all_gather(far, "tensor", axis_index_groups=FAR, axis=1, tiled=True)
    q_blocks, p_round = kernel_call(
        factor_kernel,
        out_shape=(shape(2 * CHIPS, 32, 128, dtype=BF16), shape(ROWS, R, dtype=BF16)),
    )(far, p_sum)
    q_mine = lax.all_to_all(q_blocks, ("dp", "tensor"), 0, 0, axis_index_groups=PAIRED)
    q_other = lax.ppermute(q_mine, "dp", SWAP)
    update, new_error, q_new = kernel_call(
        update_kernel,
        in_specs=[vmem, vmem, vmem, vmem],
        out_specs=[hbm, hbm, hbm],
        out_shape=(shape(ROWS, D, dtype=BF16), shape(1, ROWS, D, dtype=BF16), shape(R, COLS)),
        scratch_shapes=[
            pltpu.VMEM((ROWS, D), BF16),
            pltpu.VMEM((ROWS, D), BF16),
            pltpu.VMEM((R, COLS), F32),
            pltpu.SemaphoreType.DMA((2, PARTS)),
            pltpu.SemaphoreType.DMA,
        ],
    )(q_mine, q_other, p_round, corrected)
    return (update, new_error, q_new.T)


def solution(mesh):
    placed = (P("dp", "tensor", None), P("dp", "tensor", None), P("tensor", None))
    return jax.shard_map(
        body,
        mesh=mesh,
        in_specs=placed,
        out_specs=(P("tensor", None), P("dp", "tensor", None), P("tensor", None)),
        check_vma=False,
    )
```

```python
import jax
import jax.numpy as jnp
from jax import lax
from jax.experimental import pallas as pl
from jax.experimental.pallas import tpu as pltpu
from jax.sharding import PartitionSpec as P

SIDE = 4
CHIPS = SIDE * SIDE
CORES = 2
DP = CHIPS * CORES
DEPTH = 16
ROWS = 128
HALF = ROWS // CORES
D = 4096
COLS = D // CHIPS
R = 64
GRAM = 24
PARTS = 4
HIGH = lax.Precision.HIGHEST
F32, BF16 = jnp.float32, jnp.bfloat16

PLANE = [[core + CORES * chip for chip in range(CHIPS)] for core in range(CORES)]
NEAR = [[4 * a + b for b in range(4)] for a in range(4)]
FAR = [[4 * a + b for a in range(4)] for b in range(4)]
SWAP = [(i, i ^ 1) for i in range(DP)]
PAIRED = [
    [(CORES * k + core) * DEPTH + 2 * a + b for b in range(2) for k in range(CHIPS)]
    for a in range(DEPTH // 2)
    for core in range(CORES)
]


def ring(a, b, n):
    return min((a - b) % n, (b - a) % n)


def factor_route():
    pairs = []
    for k in range(CHIPS):
        planes = sorted(range(DEPTH), key=lambda z: -ring(z, k, DEPTH))
        chips = sorted(
            range(CHIPS),
            key=lambda j: ring(j // SIDE, k // SIDE, SIDE) + ring(j % SIDE, k % SIDE, SIDE),
        )
        for z, j in zip(planes, chips):
            for core in range(CORES):
                pairs.append(((CORES * j + core) * DEPTH + k, (CORES * k + core) * DEPTH + z))
    return pairs


def shape(*dims, dtype=F32):
    return jax.ShapeDtypeStruct(dims, dtype)


def pack(x):
    return jnp.concatenate([x[:32, :R], x[32:, :R]], 1)


def fold(gram):
    corners = (gram[:32, :32], gram[:32, 32:], gram[32:, 32:])
    return jnp.concatenate(
        [jnp.concatenate([x[8 * n : 8 * n + 8] for n in range(4)], 1) for x in corners], 0
    )


def unfold(x):
    a, b, c = (
        jnp.concatenate([x[8 * m : 8 * m + 8, 32 * n : 32 * n + 32] for n in range(4)], 0)
        for m in range(3)
    )
    upper = jnp.concatenate([jnp.concatenate([a, b], 1), jnp.concatenate([jnp.zeros_like(b), c], 1)], 0)
    rows = lax.broadcasted_iota(jnp.int32, (R, R), 0)
    return jnp.where((rows >= 32) & (lax.broadcasted_iota(jnp.int32, (R, R), 1) < 32), upper.T, upper)


def unpack(x):
    return jnp.concatenate([x[:, :R], x[:, R:]], 0)


def dot(a, b, over, **kw):
    return lax.dot_general(a, b, (over, ((), ())), preferred_element_type=F32, **kw)


def block_kernel(grad_ref, error_ref, out_ref, grad_in, error_in, blocks, in_sems, out_sems):
    size = ROWS // PARTS

    def arrivals(n):
        rows = pl.ds(n * size, size)
        return [
            pltpu.make_async_copy(grad_ref.at[0, rows], grad_in.at[rows], in_sems.at[0, n]),
            pltpu.make_async_copy(error_ref.at[0, rows], error_in.at[rows], in_sems.at[1, n]),
        ]

    def departure(c):
        return pltpu.make_async_copy(blocks.at[:, c], out_ref.at[:, c], out_sems.at[c])

    for n in range(PARTS):
        for copy in arrivals(n):
            copy.start()
    for n in range(PARTS):
        for copy in arrivals(n):
            copy.wait()
        c, row = divmod(n * size, HALF)
        rows = slice(n * size, (n + 1) * size)
        for k in range(CHIPS):
            span = slice(COLS * k, COLS * (k + 1))
            x = grad_in[rows, span].astype(F32) + error_in[rows, span].astype(F32)
            blocks[k, c, row : row + size] = x.astype(BF16)
        if row + size == HALF:
            departure(c).start()
    for c in range(CORES):
        departure(c).wait()


def sketch_kernel(blocks_ref, factor_ref, total_ref, share_ref):
    total = blocks_ref[0].astype(F32)
    for i in range(1, DP):
        total = total + blocks_ref[i].astype(F32)
    total_ref[...] = total
    part = pack(dot(total, factor_ref[...].astype(F32), ((1,), (1,)), precision=HIGH))
    share_ref[...] = jnp.broadcast_to(part[None], share_ref.shape)


def basis_kernel(share_ref, total_ref, give_ref, keep_ref):
    packed = share_ref[0]
    for k in range(1, CHIPS):
        packed = packed + share_ref[k]
    p = unpack(packed)
    first = lax.rem(lax.axis_index("dp"), CORES) == 0
    left = dot(p, total_ref[:, :128], ((0,), (0,)), precision=HIGH)
    right = dot(p, total_ref[:, 128:], ((0,), (0,)), precision=HIGH)
    gram = fold(dot(p, p, ((0,), (0,)), precision=HIGH))
    keep_ref[:R] = jnp.where(first, left, right)
    give_ref[:R] = jnp.where(first, right, left)
    for ref in (keep_ref, give_ref):
        ref[R : R + GRAM] = gram
        ref[R + GRAM :] = packed


def near_kernel(keep_ref, got_ref, share_ref, p_ref):
    both = keep_ref[:R] + got_ref[:R]
    gram = keep_ref[R : R + GRAM] + got_ref[R : R + GRAM]
    for half in range(2):
        part = pack(both[:, R * half : R * (half + 1)])
        for m in (half, half + 2):
            share_ref[m, :32] = part
            share_ref[m, 32:] = gram
    first = lax.rem(lax.axis_index("dp"), CORES) == 0
    mine, other = unpack(keep_ref[R + GRAM :]), unpack(got_ref[R + GRAM :])
    p_ref[:HALF] = jnp.where(first, mine, other)
    p_ref[HALF:] = jnp.where(first, other, mine)


def far_kernel(near_ref, share_ref):
    share_ref[...] = near_ref[0] + near_ref[1] + (near_ref[2] + near_ref[3])


def splat_row(x, row):
    return jnp.broadcast_to(x[row : row + 1, :], (8, 128))


def inverse_factor(gram):
    rows = lax.broadcasted_iota(jnp.int32, (R, R), 0)
    eye = (rows == lax.broadcasted_iota(jnp.int32, (R, R), 1)).astype(F32)
    both = jnp.concatenate([gram, eye], 1)
    n = R // 8
    strips = [both[8 * t : 8 * t + 8] for t in range(n)]
    sub = lax.broadcasted_iota(jnp.int32, (8, 128), 0)
    scaled = []
    for s in range(n):
        cols = [
            [jnp.broadcast_to(strips[t][:, 8 * s + j : 8 * s + j + 1], (8, 128)) for t in range(s, n)]
            for j in range(8)
        ]
        done = jnp.zeros((8, 128), F32)
        for j in range(8):
            pivot, row = splat_row(cols[j][0], j), splat_row(strips[s], j)
            root = lax.rsqrt(pivot)
            done = jnp.where(sub == j, row * root, done)
            inverse = 1.0 / pivot
            factors = [c * inverse for c in cols[j]]
            factors[0] = jnp.where(sub > j, factors[0], 0.0)
            for i in range(j + 1, 8):
                entry = splat_row(cols[i][0], j)
                cols[i] = [c - f * entry for c, f in zip(cols[i], factors)]
            for t in range(s, n):
                strips[t] = strips[t] - factors[t - s] * row
        scaled.append(done)
    return jnp.concatenate(scaled, 0)[:, R:]


def factor_kernel(far_ref, p_ref, q_ref, p_round_ref):
    both = far_ref[:, :128] + far_ref[:, 128:256] + (far_ref[:, 256:384] + far_ref[:, 384:])
    inverse = inverse_factor(unfold(both[32:]))
    q_half = dot(inverse, unpack(both[:32]), ((1,), (0,)), precision=HIGH) * (1.0 / DP)
    q_ref[...] = jnp.broadcast_to(pack(q_half).astype(BF16)[None], q_ref.shape)
    p_round_ref[...] = dot(p_ref[...], inverse, ((1,), (1,)), precision=HIGH).astype(BF16)


def update_kernel(
    mine_ref, other_ref, p_ref, rows_ref, update_ref, error_ref, q_new_ref, update_out, error_out, q_new_out, sems, q_sem
):
    width = D // PARTS
    z = lax.axis_index("tensor")
    first = lax.rem(lax.axis_index("dp"), CORES) == 0

    def block(k, c):
        even, odd = (
            jnp.where(first if c == 0 else ~first, mine_ref[n + k], other_ref[n + k])
            for n in (0, CHIPS)
        )
        upper = jnp.concatenate([even[:, :R], odd[:, :R]], 1)
        lower = jnp.concatenate([even[:, R:], odd[:, R:]], 1)
        return jnp.concatenate([upper, lower], 0)

    def copies(n):
        span = pl.ds(n * width, width)
        return [
            pltpu.make_async_copy(update_out.at[:, span], update_ref.at[:, span], sems.at[0, n]),
            pltpu.make_async_copy(error_out.at[:, span], error_ref.at[0, :, span], sems.at[1, n]),
        ]

    for n in range(PARTS):
        for k in range(n * width // COLS, (n + 1) * width // COLS):
            q = jnp.concatenate([block(k, c) for c in range(CORES)], 1)
            full = dot(p_ref[...], q, ((1,), (0,)))
            span = slice(COLS * k, COLS * (k + 1))
            update_out[:, span] = full.astype(BF16)
            error_out[:, span] = (rows_ref[:, span].astype(F32) - full).astype(BF16)
        for copy in copies(n):
            copy.start()
    for c in range(CORES):
        q_new_out[:, 128 * c : 128 * (c + 1)] = block(z, c).astype(F32)
    q_copy = pltpu.make_async_copy(q_new_out, q_new_ref, q_sem)
    q_copy.start()
    for n in range(PARTS):
        for copy in copies(n):
            copy.wait()
    q_copy.wait()


def kernel_call(kernel, mib=4, **kw):
    return pl.pallas_call(
        kernel, compiler_params=pltpu.CompilerParams(vmem_limit_bytes=mib << 20), **kw
    )


def body(grad, error, q_start):
    vmem, hbm = pl.BlockSpec(memory_space=pltpu.VMEM), pl.BlockSpec(memory_space=pltpu.HBM)
    factor_t = lax.ppermute(q_start.T, ("dp", "tensor"), factor_route())
    corrected = (grad[0].astype(F32) + error[0].astype(F32)).astype(BF16)
    blocks = kernel_call(
        block_kernel,
        mib=56,
        in_specs=[hbm, hbm],
        out_specs=hbm,
        out_shape=shape(CHIPS, CORES, HALF, COLS, dtype=BF16),
        scratch_shapes=[
            pltpu.VMEM((ROWS, D), BF16),
            pltpu.VMEM((ROWS, D), BF16),
            pltpu.VMEM((CHIPS, CORES, HALF, COLS), BF16),
            pltpu.SemaphoreType.DMA((2, PARTS)),
            pltpu.SemaphoreType.DMA((CORES,)),
        ],
    )(grad, error)
    blocks = lax.all_to_all(blocks.reshape(DP, HALF, COLS), "dp", 0, 0)
    total, part = kernel_call(
        sketch_kernel, out_shape=(shape(HALF, COLS), shape(CHIPS, 32, 128))
    )(blocks, factor_t)
    part = lax.all_to_all(part, "dp", 0, 0, axis_index_groups=PLANE)
    give, keep = kernel_call(basis_kernel, out_shape=(shape(R + GRAM + 32, 128),) * 2)(part, total)
    got = lax.ppermute(give, "dp", SWAP)
    near, p_sum = kernel_call(near_kernel, out_shape=(shape(4, 32 + GRAM, 128), shape(ROWS, R)))(keep, got)
    near = lax.all_to_all(near, "tensor", 0, 0, axis_index_groups=NEAR)
    far = kernel_call(far_kernel, out_shape=shape(32 + GRAM, 128))(near)
    far = lax.all_gather(far, "tensor", axis_index_groups=FAR, axis=1, tiled=True)
    q_blocks, p_round = kernel_call(
        factor_kernel,
        out_shape=(shape(2 * CHIPS, 32, 128, dtype=BF16), shape(ROWS, R, dtype=BF16)),
    )(far, p_sum)
    q_mine = lax.all_to_all(q_blocks, ("dp", "tensor"), 0, 0, axis_index_groups=PAIRED)
    q_other = lax.ppermute(q_mine, "dp", SWAP)
    update, new_error, q_new = kernel_call(
        update_kernel,
        in_specs=[vmem, vmem, vmem, vmem],
        out_specs=[hbm, hbm, hbm],
        out_shape=(shape(ROWS, D, dtype=BF16), shape(1, ROWS, D, dtype=BF16), shape(R, COLS)),
        scratch_shapes=[
            pltpu.VMEM((ROWS, D), BF16),
            pltpu.VMEM((ROWS, D), BF16),
            pltpu.VMEM((R, COLS), F32),
            pltpu.SemaphoreType.DMA((2, PARTS)),
            pltpu.SemaphoreType.DMA,
        ],
    )(q_mine, q_other, p_round, corrected)
    return (update, new_error, q_new.T)


def solution(mesh):
    placed = (P("dp", "tensor", None), P("dp", "tensor", None), P("tensor", None))
    return jax.shard_map(
        body,
        mesh=mesh,
        in_specs=placed,
        out_specs=(P("tensor", None), P("dp", "tensor", None), P("tensor", None)),
        check_vma=False,
    )
```

```python
import jax
import jax.numpy as jnp
from jax import lax
from jax.experimental import pallas as pl
from jax.experimental.pallas import tpu as pltpu
from jax.sharding import PartitionSpec as P

SIDE = 4
CHIPS = SIDE * SIDE
CORES = 2
DP = CHIPS * CORES
DEPTH = 16
ROWS = 128
HALF = ROWS // CORES
D = 4096
COLS = D // CHIPS
R = 64
GRAM = 24
WRITES = 8
PARTS = 4
HIGH = lax.Precision.HIGHEST
F32, BF16 = jnp.float32, jnp.bfloat16

PLANE = [[core + CORES * chip for chip in range(CHIPS)] for core in range(CORES)]
NEAR = [[4 * a + b for b in range(4)] for a in range(4)]
FAR = [[4 * a + b for a in range(4)] for b in range(4)]
SWAP = [(i, i ^ 1) for i in range(DP)]
PAIRED = [
    [(CORES * k + core) * DEPTH + 2 * a + b for b in range(2) for k in range(CHIPS)]
    for a in range(DEPTH // 2)
    for core in range(CORES)
]


def ring(a, b, n):
    return min((a - b) % n, (b - a) % n)


def factor_route():
    pairs = []
    for k in range(CHIPS):
        planes = sorted(range(DEPTH), key=lambda z: -ring(z, k, DEPTH))
        chips = sorted(
            range(CHIPS),
            key=lambda j: ring(j // SIDE, k // SIDE, SIDE) + ring(j % SIDE, k % SIDE, SIDE),
        )
        for z, j in zip(planes, chips):
            for core in range(CORES):
                pairs.append(((CORES * j + core) * DEPTH + k, (CORES * k + core) * DEPTH + z))
    return pairs


def shape(*dims, dtype=F32):
    return jax.ShapeDtypeStruct(dims, dtype)


def pack(x):
    return jnp.concatenate([x[:32, :R], x[32:, :R]], 1)


def fold(gram):
    corners = (gram[:32, :32], gram[:32, 32:], gram[32:, 32:])
    return jnp.concatenate(
        [jnp.concatenate([x[8 * n : 8 * n + 8] for n in range(4)], 1) for x in corners], 0
    )


def unfold(x):
    a, b, c = (
        jnp.concatenate([x[8 * m : 8 * m + 8, 32 * n : 32 * n + 32] for n in range(4)], 0)
        for m in range(3)
    )
    upper = jnp.concatenate([jnp.concatenate([a, b], 1), jnp.concatenate([jnp.zeros_like(b), c], 1)], 0)
    rows = lax.broadcasted_iota(jnp.int32, (R, R), 0)
    return jnp.where((rows >= 32) & (lax.broadcasted_iota(jnp.int32, (R, R), 1) < 32), upper.T, upper)


def unpack(x):
    return jnp.concatenate([x[:, :R], x[:, R:]], 0)


def dot(a, b, over, **kw):
    return lax.dot_general(a, b, (over, ((), ())), preferred_element_type=F32, **kw)


def block_kernel(grad_ref, error_ref, out_ref, grad_in, error_in, blocks, in_sems, out_sems):
    size = ROWS // PARTS

    def arrivals(n):
        rows = pl.ds(n * size, size)
        return [
            pltpu.make_async_copy(grad_ref.at[0, rows], grad_in.at[rows], in_sems.at[0, n]),
            pltpu.make_async_copy(error_ref.at[0, rows], error_in.at[rows], in_sems.at[1, n]),
        ]

    def departure(c):
        return pltpu.make_async_copy(blocks.at[:, c], out_ref.at[:, c], out_sems.at[c])

    for n in range(PARTS):
        for copy in arrivals(n):
            copy.start()
    for n in range(PARTS):
        for copy in arrivals(n):
            copy.wait()
        c, row = divmod(n * size, HALF)
        rows = slice(n * size, (n + 1) * size)
        for k in range(CHIPS):
            span = slice(COLS * k, COLS * (k + 1))
            x = grad_in[rows, span].astype(F32) + error_in[rows, span].astype(F32)
            blocks[k, c, row : row + size] = x.astype(BF16)
        if row + size == HALF:
            departure(c).start()
    for c in range(CORES):
        departure(c).wait()


def sketch_kernel(blocks_ref, factor_ref, total_ref, share_ref):
    total = blocks_ref[0].astype(F32)
    for i in range(1, DP):
        total = total + blocks_ref[i].astype(F32)
    total_ref[...] = total
    part = pack(dot(total, factor_ref[...].astype(F32), ((1,), (1,)), precision=HIGH))
    share_ref[...] = jnp.broadcast_to(part[None], share_ref.shape)


def basis_kernel(share_ref, total_ref, give_ref, keep_ref):
    packed = share_ref[0]
    for k in range(1, CHIPS):
        packed = packed + share_ref[k]
    p = unpack(packed)
    first = lax.rem(lax.axis_index("dp"), CORES) == 0
    left = dot(p, total_ref[:, :128], ((0,), (0,)), precision=HIGH)
    right = dot(p, total_ref[:, 128:], ((0,), (0,)), precision=HIGH)
    gram = fold(dot(p, p, ((0,), (0,)), precision=HIGH))
    keep_ref[:R] = jnp.where(first, left, right)
    give_ref[:R] = jnp.where(first, right, left)
    for ref in (keep_ref, give_ref):
        ref[R : R + GRAM] = gram
        ref[R + GRAM :] = packed


def near_kernel(keep_ref, got_ref, share_ref, p_ref):
    both = keep_ref[:R] + got_ref[:R]
    gram = keep_ref[R : R + GRAM] + got_ref[R : R + GRAM]
    for half in range(2):
        part = pack(both[:, R * half : R * (half + 1)])
        for m in (half, half + 2):
            share_ref[m, :32] = part
            share_ref[m, 32:] = gram
    first = lax.rem(lax.axis_index("dp"), CORES) == 0
    mine, other = unpack(keep_ref[R + GRAM :]), unpack(got_ref[R + GRAM :])
    p_ref[:HALF] = jnp.where(first, mine, other)
    p_ref[HALF:] = jnp.where(first, other, mine)


def far_kernel(near_ref, share_ref):
    share_ref[...] = near_ref[0] + near_ref[1] + (near_ref[2] + near_ref[3])


def splat_row(x, row):
    return jnp.broadcast_to(x[row : row + 1, :], (8, 128))


def inverse_factor(gram):
    rows = lax.broadcasted_iota(jnp.int32, (R, R), 0)
    eye = (rows == lax.broadcasted_iota(jnp.int32, (R, R), 1)).astype(F32)
    both = jnp.concatenate([gram, eye], 1)
    n = R // 8
    strips = [both[8 * t : 8 * t + 8] for t in range(n)]
    sub = lax.broadcasted_iota(jnp.int32, (8, 128), 0)
    scaled = []
    for s in range(n):
        cols = [
            [jnp.broadcast_to(strips[t][:, 8 * s + j : 8 * s + j + 1], (8, 128)) for t in range(s, n)]
            for j in range(8)
        ]
        done = jnp.zeros((8, 128), F32)
        for j in range(8):
            pivot, row = splat_row(cols[j][0], j), splat_row(strips[s], j)
            root = lax.rsqrt(pivot)
            done = jnp.where(sub == j, row * root, done)
            factors = [c * (root * root) for c in cols[j]]
            factors[0] = jnp.where(sub > j, factors[0], 0.0)
            for i in range(j + 1, 8):
                entry = splat_row(cols[i][0], j)
                cols[i] = [c - f * entry for c, f in zip(cols[i], factors)]
            for t in range(s, n):
                strips[t] = strips[t] - factors[t - s] * row
        scaled.append(done)
    return jnp.concatenate(scaled, 0)[:, R:]


def factor_kernel(far_ref, p_ref, q_ref, p_round_ref):
    both = far_ref[:, :128] + far_ref[:, 128:256] + (far_ref[:, 256:384] + far_ref[:, 384:])
    inverse = inverse_factor(unfold(both[32:]))
    q_half = dot(inverse, unpack(both[:32]), ((1,), (0,)), precision=HIGH) * (1.0 / DP)
    q_ref[...] = jnp.broadcast_to(pack(q_half).astype(BF16)[None], q_ref.shape)
    p_round_ref[...] = dot(p_ref[...], inverse, ((1,), (1,)), precision=HIGH).astype(BF16)


def update_kernel(
    mine_ref, other_ref, p_ref, rows_ref, update_ref, error_ref, q_new_ref, update_out, error_out, q_new_out, sems, q_sem
):
    width = D // WRITES
    z = lax.axis_index("tensor")
    first = lax.rem(lax.axis_index("dp"), CORES) == 0

    def block(k, c):
        even, odd = (
            jnp.where(first if c == 0 else ~first, mine_ref[n + k], other_ref[n + k])
            for n in (0, CHIPS)
        )
        upper = jnp.concatenate([even[:, :R], odd[:, :R]], 1)
        lower = jnp.concatenate([even[:, R:], odd[:, R:]], 1)
        return jnp.concatenate([upper, lower], 0)

    for c in range(CORES):
        q_new_out[:, 128 * c : 128 * (c + 1)] = block(z, c).astype(F32)
    q_copy = pltpu.make_async_copy(q_new_out, q_new_ref, q_sem)
    q_copy.start()

    def copies(n):
        span = pl.ds(n * width, width)
        return [
            pltpu.make_async_copy(update_out.at[:, span], update_ref.at[:, span], sems.at[0, n]),
            pltpu.make_async_copy(error_out.at[:, span], error_ref.at[0, :, span], sems.at[1, n]),
        ]

    for n in range(WRITES):
        for k in range(n * width // COLS, (n + 1) * width // COLS):
            q = jnp.concatenate([block(k, c) for c in range(CORES)], 1)
            full = dot(p_ref[...], q, ((1,), (0,)))
            span = slice(COLS * k, COLS * (k + 1))
            update_out[:, span] = full.astype(BF16)
            error_out[:, span] = (rows_ref[:, span].astype(F32) - full).astype(BF16)
        for copy in copies(n):
            copy.start()
    for n in range(WRITES):
        for copy in copies(n):
            copy.wait()
    q_copy.wait()


def kernel_call(kernel, mib=4, **kw):
    return pl.pallas_call(
        kernel, compiler_params=pltpu.CompilerParams(vmem_limit_bytes=mib << 20), **kw
    )


def body(grad, error, q_start):
    vmem, hbm = pl.BlockSpec(memory_space=pltpu.VMEM), pl.BlockSpec(memory_space=pltpu.HBM)
    factor_t = lax.ppermute(q_start.T, ("dp", "tensor"), factor_route())
    corrected = (grad[0].astype(F32) + error[0].astype(F32)).astype(BF16)
    blocks = kernel_call(
        block_kernel,
        mib=56,
        in_specs=[hbm, hbm],
        out_specs=hbm,
        out_shape=shape(CHIPS, CORES, HALF, COLS, dtype=BF16),
        scratch_shapes=[
            pltpu.VMEM((ROWS, D), BF16),
            pltpu.VMEM((ROWS, D), BF16),
            pltpu.VMEM((CHIPS, CORES, HALF, COLS), BF16),
            pltpu.SemaphoreType.DMA((2, PARTS)),
            pltpu.SemaphoreType.DMA((CORES,)),
        ],
    )(grad, error)
    blocks = lax.all_to_all(blocks.reshape(DP, HALF, COLS), "dp", 0, 0)
    total, part = kernel_call(
        sketch_kernel, out_shape=(shape(HALF, COLS), shape(CHIPS, 32, 128))
    )(blocks, factor_t)
    part = lax.all_to_all(part, "dp", 0, 0, axis_index_groups=PLANE)
    give, keep = kernel_call(basis_kernel, out_shape=(shape(R + GRAM + 32, 128),) * 2)(part, total)
    got = lax.ppermute(give, "dp", SWAP)
    near, p_sum = kernel_call(near_kernel, out_shape=(shape(4, 32 + GRAM, 128), shape(ROWS, R)))(keep, got)
    near = lax.all_to_all(near, "tensor", 0, 0, axis_index_groups=NEAR)
    far = kernel_call(far_kernel, out_shape=shape(32 + GRAM, 128))(near)
    far = lax.all_gather(far, "tensor", axis_index_groups=FAR, axis=1, tiled=True)
    q_blocks, p_round = kernel_call(
        factor_kernel,
        out_shape=(shape(2 * CHIPS, 32, 128, dtype=BF16), shape(ROWS, R, dtype=BF16)),
    )(far, p_sum)
    q_mine = lax.all_to_all(q_blocks, ("dp", "tensor"), 0, 0, axis_index_groups=PAIRED)
    q_other = lax.ppermute(q_mine, "dp", SWAP)
    update, new_error, q_new = kernel_call(
        update_kernel,
        in_specs=[vmem, vmem, vmem, vmem],
        out_specs=[hbm, hbm, hbm],
        out_shape=(shape(ROWS, D, dtype=BF16), shape(1, ROWS, D, dtype=BF16), shape(R, COLS)),
        scratch_shapes=[
            pltpu.VMEM((ROWS, D), BF16),
            pltpu.VMEM((ROWS, D), BF16),
            pltpu.VMEM((R, COLS), F32),
            pltpu.SemaphoreType.DMA((2, WRITES)),
            pltpu.SemaphoreType.DMA,
        ],
    )(q_mine, q_other, p_round, corrected)
    return (update, new_error, q_new.T)


def solution(mesh):
    placed = (P("dp", "tensor", None), P("dp", "tensor", None), P("tensor", None))
    return jax.shard_map(
        body,
        mesh=mesh,
        in_specs=placed,
        out_specs=(P("tensor", None), P("dp", "tensor", None), P("tensor", None)),
        check_vma=False,
    )
```
